32 devices in a mesh: row: 8 (over z, y), col: 4 (over x, core).
Axes of the slice: x: 2, y: 2, z: 4, core: 2. Of those that a mesh axis runs over, the one named last changes fastest.
Arguments:
- center: bfloat16 [512, 8192], P('col', 'row'), may hold values from -6 to 6
- radius: bfloat16 [512, 8192], P('col', 'row'), may hold values from 0.049804688 to 1
- grad_center: bfloat16 [512, 8192], P('row', 'col'), may hold values from -6 to 6
- grad_radius: bfloat16 [512, 8192], P('row', 'col'), may hold values from -6 to 6
- weight: bfloat16 [8192, 8192], P('row', 'col'), may hold values from -0.0625 to 0.0625
- active: int32 [512, 8192], P('col', 'row'), may hold values 0 or 1
Outputs:
- center_in: float32 [512, 8192], P('col', 'row')
- radius_in: float32 [512, 8192], P('col', 'row')
- weight_grad: float32 [8192, 8192], P('row', 'col')
The draws below stay inside these ranges and needn't reach their ends.
All inputs are finite; a program needn't handle non-finite values. No bound on the sum of `active` on one device may be relied on, other than what follows from the above.
Results may differ from the reference program's by a relative error of at most 0.0003.
Values may be sent and summed in bfloat16 or wider, within the bound.
No kernel may reach another device: no remote copies, remote signals or barrier semaphores. Data moves between devices by JAX's collectives and lax.ppermute only.
A program may use at most 64 MiB of HBM per device.

```python
import jax
import jax.numpy as jnp

D = 8192
INNER = 8192
TOK = 512


def plant(array, rng, low, top_value):
    index_at = [jax.random.randint(jax.random.fold_in(rng, axis), (), 0, length) for axis, length in enumerate(array.shape)]
    widest = array.shape.index(max(array.shape))
    next_to = index_at[:widest] + [(index_at[widest] + 1) % array.shape[widest]] + index_at[widest + 1:]
    return array.at[tuple(index_at)].set(low).at[tuple(next_to)].set(top_value)


def spiked(drawn, key, source, target, shards_of, factor):
    def block_of(position):
        return (jnp.arange(drawn.shape[position]) // (drawn.shape[position] // shards_of)).reshape((-1,) + (1,) * (drawn.ndim - 1 - position))

    first = jax.random.permutation(key, shards_of)[block_of(target)]
    far = (block_of(target) + shards_of // 2) % shards_of
    return jnp.where((block_of(source) == first) | (block_of(source) == far), factor * drawn, drawn)


def shard_levels(own_key, extent, split, smallest, largest):
    def one(dim, parts):
        draws = jax.random.uniform(jax.random.fold_in(jax.random.fold_in(own_key, 6), dim), (parts,), jnp.float32, smallest / len(split), largest / len(split))
        return jnp.repeat(jnp.exp(draws), extent[dim] // parts).reshape((-1,) + (1,) * (len(extent) - dim - 1))

    loudness = one(*split[0])
    for cut in split[1:]:
        loudness = loudness * one(*cut)
    return loudness


def scatter_about(key, extent, scale, most, split=(), dtype=jnp.bfloat16):
    drawn = jax.random.normal(key, extent, jnp.float32) * scale
    if len(split) > 0:
        drawn = shard_levels(key, extent, split, -0.22, 0.18) * drawn
    return jnp.clip(drawn, min=-most, max=most).astype(dtype)


def bell_draw_with(stream_key, dims, scale, bound, cuts, heavy, kind=jnp.bfloat16):
    drawn = scale * jax.random.normal(stream_key, dims, jnp.float32)
    if cuts:
        drawn = drawn * shard_levels(stream_key, dims, cuts, -0.22, 0.18)
    return jnp.clip(spiked(drawn, jax.random.fold_in(stream_key, 3), *heavy), -bound, bound).astype(kind)


def setup_inputs(seed: int = 0) -> dict:
    splits = jax.random.split(jax.random.key(seed), 7)
    return {
        "center": scatter_about(splits[0], (TOK, INNER), 1.0, 6.0, ((0, 4), (1, 8))),
        "radius": jnp.clip(0.049804688 + 0.9501953 * jax.random.uniform(splits[1], (TOK, INNER), jnp.float32) ** shard_levels(splits[1], (TOK, INNER), ((0, 4), (1, 8)), -0.2, 0.2), 0.049804688, 1.0).astype(jnp.bfloat16),
        "grad_center": bell_draw_with(splits[2], (TOK, D), 1.0, 6.0, ((0, 8), (1, 4)), (1, 0, 8, 2.0)),
        "grad_radius": bell_draw_with(splits[3], (TOK, D), 1.0, 6.0, ((0, 8), (1, 4)), (1, 0, 8, 2.0)),
        "weight": scatter_about(splits[4], (INNER, D), INNER ** -0.5, 0.0625, ((0, 8), (1, 4))),
        "active": plant((jax.random.randint(splits[5], (TOK, INNER), 0, 4) < 3).astype(jnp.int32), jax.random.fold_in(splits[5], 1), 0, 1),
    }


def reference(center, radius, grad_center, grad_radius, weight, active):
    magnitude = jnp.abs(weight)
    gating = active.astype(jnp.float32)
    center_sum = jnp.dot(grad_center, weight.T, preferred_element_type=jnp.float32)
    radius_sum = jnp.dot(grad_radius, magnitude.T, preferred_element_type=jnp.float32)
    center_in = gating * center_sum
    radius_in = gating * radius_sum
    center_part = jnp.dot(center.T, grad_center, preferred_element_type=jnp.float32)
    radius_part = jnp.dot(radius.T, grad_radius, preferred_element_type=jnp.float32)
    scale_factor = jnp.float32(1.0) / jnp.sqrt(jnp.float32(TOK))
    weight_grad = (center_part + jnp.sign(weight).astype(jnp.float32) * radius_part) * scale_factor
    return (center_in, radius_in, weight_grad)
```

```python
import functools

import jax
import jax.numpy as jnp
import numpy as np
from jax import lax
from jax.experimental import pallas as pl
from jax.experimental.pallas import tpu as pltpu
from jax.sharding import PartitionSpec as P

VMEM_LIMIT = 24 * 1024 * 1024
VMEM_ALL = 60 * 1024 * 1024
VMEM_MOST = 48 * 1024 * 1024
HERE = pl.BlockSpec(memory_space=pltpu.VMEM)
LANES = 128
LEVELS = np.float32(32000)
TINY = np.float32(2.0**-100)
ANYWHERE = pl.BlockSpec(memory_space=pl.ANY)
BY_LAST = (((1,), (1,)), ((), ()))
BY_TOKEN = (((1,), (0,)), ((), ()))


def ring_of(rows):
    if rows % 2:
        return list(range(rows))
    return list(range(0, rows, 2)) + list(range(rows - 1, 0, -2))


def on_ring(row, rows):
    return row if rows % 2 else lax.select(lax.rem(row, 2) == 0, lax.div(row, 2), rows - 1 - lax.div(row, 2))


def off_ring(place, rows):
    return place if rows % 2 else lax.select(place < rows // 2, 2 * place, 2 * (rows - place) - 1)


def col_split(cols):
    return (cols // 2, 2) if cols % 2 == 0 else (cols, 1)


def place(rows, cols, owned, shifts, slots, half, held, order):
    chips, cores = col_split(cols)
    here, col = on_ring(lax.axis_index("row"), rows), lax.axis_index("col")
    x, core = lax.div(col, cores), lax.rem(col, cores)
    share = owned // held
    for shift, slot in zip(shifts, slots):
        first = half * held if slot.shape[0] > held else 0
        source = off_ring(lax.rem(here + (rows - shift) % rows, rows), rows)
        owner = lax.div(source, share)
        away = lax.rem(lax.rem(owner, cores) + cores - core, cores)
        near = away * chips + lax.rem(lax.div(owner, cores) + chips - x, chips)
        start = pl.multiple_of((near * share + lax.rem(source, share)) * held, held)
        order[pl.ds(start, held), :] = slot[first : first + held, :]


def input_kernel(rows, cols, shifts, absolute, *refs):
    count, pieces = len(shifts), cols
    slots, weight, outs, order = refs[:count], refs[count], refs[count + 1 : -1], refs[-1]
    inner = weight.shape[0]
    tile = min(256, inner)
    step = order.shape[0] // pieces
    place(rows, cols, step, shifts, slots, int(absolute), order.shape[0] // rows, order)
    for i in range(inner // tile):
        span = slice(i * tile, (i + 1) * tile)
        block = weight[span, :]
        if absolute:
            block = jnp.abs(block)
        terms = lax.dot_general(order[...], block, BY_LAST, preferred_element_type=jnp.float32)
        for n in range(pieces):
            outs[n][:, span] = terms[n * step : (n + 1) * step, :]


def input_terms(rows, cols, shifts, slots, weight, absolute):
    inner, width = weight.shape
    tokens = slots[0].shape[0] // 2 * rows
    found = pl.pallas_call(
        functools.partial(input_kernel, rows, cols, shifts, absolute),
        in_specs=[HERE] * (len(slots) + 1),
        out_specs=[HERE] * (cols + 1),
        out_shape=[jax.ShapeDtypeStruct((tokens // cols, inner), jnp.float32)] * cols
        + [jax.ShapeDtypeStruct((tokens, width), jnp.bfloat16)],
        compiler_params=pltpu.CompilerParams(vmem_limit_bytes=VMEM_LIMIT),
        cost_estimate=pl.CostEstimate(
            flops=2 * tokens * inner * width,
            bytes_accessed=2 * (tokens + inner) * width + 4 * tokens * inner,
            transcendentals=0,
        ),
    )(*slots, weight)
    return found[:cols], found[cols]


def load_kernel(source, target, sem):
    copy = pltpu.make_async_copy(source, target, sem)
    copy.start()
    copy.wait()


def loaded(value):
    return pl.pallas_call(
        load_kernel,
        in_specs=[ANYWHERE],
        out_specs=HERE,
        out_shape=jax.ShapeDtypeStruct(value.shape, value.dtype),
        scratch_shapes=[pltpu.SemaphoreType.DMA],
        compiler_params=pltpu.CompilerParams(vmem_limit_bytes=VMEM_MOST),
        cost_estimate=pl.CostEstimate(flops=0, bytes_accessed=4 * value.size, transcendentals=0),
    )(value)


def sum_kernel(count, *refs):
    parts, out = refs[:count], refs[count]
    total = parts[0][...]
    for part in parts[1:]:
        total = total + part[...]
    rows, width = total.shape
    most = jnp.max(jnp.abs(total), axis=1, keepdims=True)
    exponent = jnp.ceil(jnp.log2(jnp.maximum(most, TINY)) + 1e-3)
    coded = jnp.round(total * (LEVELS / jnp.exp2(exponent)))
    out[:, :width] = coded.astype(jnp.int16)
    out[:, width:] = jnp.broadcast_to(exponent, (rows, LANES)).astype(jnp.int16)


def coded_sum(*parts):
    rows, width = parts[0].shape
    return pl.pallas_call(
        functools.partial(sum_kernel, len(parts)),
        in_specs=[HERE] * len(parts),
        out_specs=HERE,
        out_shape=jax.ShapeDtypeStruct((rows, width + LANES), jnp.int16),
        compiler_params=pltpu.CompilerParams(vmem_limit_bytes=VMEM_LIMIT),
        cost_estimate=pl.CostEstimate(
            flops=4 * rows * width, bytes_accessed=10 * rows * width, transcendentals=rows
        ),
    )(*parts)


def gate_kernel(near, far, *refs):
    active, out = refs[-2:]
    width = out.shape[1]
    total = refs[0][...]
    for part in refs[1:near]:
        total = total + part[...]
    for part in refs[near : near + far]:
        exponent = part[:, width : width + 1].astype(jnp.float32)
        total = total + part[:, :width].astype(jnp.float32) * (jnp.exp2(exponent) / LEVELS)
    out[...] = active[...].astype(jnp.float32) * total


def gated(near, far, active):
    rows, width = active.shape
    return pl.pallas_call(
        functools.partial(gate_kernel, len(near), len(far)),
        in_specs=[HERE] * (len(near) + len(far) + 1),
        out_specs=HERE,
        out_shape=jax.ShapeDtypeStruct((rows, width), jnp.float32),
        compiler_params=pltpu.CompilerParams(vmem_limit_bytes=VMEM_LIMIT),
        cost_estimate=pl.CostEstimate(
            flops=8 * rows * width, bytes_accessed=20 * rows * width, transcendentals=rows
        ),
    )(*near, *far, active)


def pack_kernel(first, second, out, both, sems):
    rows = first.shape[0]
    spans = [pl.ds(0, rows), pl.ds(rows, rows)]
    copies = [
        pltpu.make_async_copy(source, both.at[span, :], sem)
        for source, span, sem in zip((first, second), spans, (sems.at[0], sems.at[1]))
    ]
    onward = [
        pltpu.make_async_copy(both.at[span, :], out.at[span, :], sem)
        for span, sem in zip(spans, (sems.at[2], sems.at[3]))
    ]
    for copy in copies:
        copy.start()
    for copy, then in zip(copies, onward):
        copy.wait()
        then.start()
    for then in onward:
        then.wait()


def packed(first, second):
    rows, width = first.shape
    return pl.pallas_call(
        pack_kernel,
        in_specs=[ANYWHERE] * 2,
        out_specs=ANYWHERE,
        out_shape=jax.ShapeDtypeStruct((2 * rows, width), first.dtype),
        scratch_shapes=[pltpu.VMEM((2 * rows, width), first.dtype), pltpu.SemaphoreType.DMA((4,))],
        compiler_params=pltpu.CompilerParams(vmem_limit_bytes=VMEM_ALL),
        cost_estimate=pl.CostEstimate(flops=0, bytes_accessed=8 * rows * width, transcendentals=0),
    )(first, second)


def turn_kernel(pieces, *refs):
    held, turned = refs[:-2], refs[-2:]
    rows = held[0].shape[0] // pieces
    tokens = 0
    for ref in held:
        for n in range(0, pieces, 2):
            for half, out in enumerate(turned):
                out[:, tokens : tokens + rows] = ref[(n + half) * rows : (n + half + 1) * rows, :].T
            tokens += rows


def turned(held, pieces):
    rows, inner = held[0].shape
    tokens = rows // 2 * len(held)
    return pl.pallas_call(
        functools.partial(turn_kernel, pieces),
        in_specs=[HERE] * len(held),
        out_specs=[HERE] * 2,
        out_shape=[jax.ShapeDtypeStruct((inner, tokens), jnp.bfloat16)] * 2,
        compiler_params=pltpu.CompilerParams(vmem_limit_bytes=VMEM_LIMIT),
        cost_estimate=pl.CostEstimate(
            flops=2 * tokens * inner, bytes_accessed=8 * tokens * inner, transcendentals=0
        ),
    )(*held)


def center_kernel(center, grads, out):
    tile = min(256, out.shape[0])

    @pl.loop(0, out.shape[0] // tile)
    def _(i):
        span = pl.ds(pl.multiple_of(i * tile, tile), tile)
        out[span, :] = lax.dot_general(
            center[span, :], grads[...], BY_TOKEN, preferred_element_type=jnp.float32
        )


def center_terms(center, grads):
    inner, tokens = center.shape
    width = grads.shape[1]
    return pl.pallas_call(
        center_kernel,
        in_specs=[HERE] * 2,
        out_specs=HERE,
        out_shape=jax.ShapeDtypeStruct((inner, width), jnp.float32),
        compiler_params=pltpu.CompilerParams(vmem_limit_bytes=VMEM_LIMIT),
        cost_estimate=pl.CostEstimate(
            flops=2 * tokens * inner * width,
            bytes_accessed=2 * tokens * (inner + width) + 4 * inner * width,
            transcendentals=0,
        ),
    )(center, grads)


def weight_kernel(scale, center, radius, grads, weight, out, parts, sems):
    tile = parts.shape[1]
    copies = []
    for n in range(out.shape[0] // tile):
        span = slice(n * tile, (n + 1) * tile)
        part, sem = parts.at[n % 2], sems.at[n % 2]
        if n >= 2:
            copies[n - 2].wait()
        through_radius = lax.dot_general(
            radius[span, :], grads[...], BY_TOKEN, preferred_element_type=jnp.float32
        )
        w = weight[span, :].astype(jnp.float32)
        signed = jnp.where(w > 0, through_radius, jnp.where(w < 0, -through_radius, 0.0))
        part[...] = (center[span, :] + signed) * scale
        copies.append(pltpu.make_async_copy(part, out.at[pl.ds(n * tile, tile), :], sem))
        copies[n].start()
    for copy in copies[-2:]:
        copy.wait()


def weight_terms(center, radius, grads, weight):
    inner, width = weight.shape
    tokens = grads.shape[0]
    tile = min(256, inner)
    scale = np.float32(1.0) / np.sqrt(np.float32(tokens))
    return pl.pallas_call(
        functools.partial(weight_kernel, scale),
        in_specs=[HERE] * 4,
        out_specs=ANYWHERE,
        out_shape=jax.ShapeDtypeStruct((inner, width), jnp.float32),
        scratch_shapes=[
            pltpu.VMEM((2, tile, width), jnp.float32),
            pltpu.SemaphoreType.DMA((2,)),
        ],
        compiler_params=pltpu.CompilerParams(vmem_limit_bytes=VMEM_LIMIT),
        cost_estimate=pl.CostEstimate(
            flops=2 * tokens * inner * width,
            bytes_accessed=2 * tokens * (inner + width) + 10 * inner * width,
            transcendentals=0,
        ),
    )(center, radius, grads, weight)


def on_device(rows, cols, center, radius, grad_center, grad_radius, weight, active):
    chips, cores = col_split(cols)
    ring = ring_of(rows)
    clockwise = [(ring[i], ring[(i + 1) % rows]) for i in range(rows)]
    counter = [(b, a) for a, b in clockwise]

    def swap_cores(value, j):
        perm = [(i, i - i % cores + (i % cores + j) % cores) for i in range(cols)]
        return lax.ppermute(value, "col", perm)

    def hop_chips(value, k):
        return lax.ppermute(value, "col", [(i, (i + k * cores) % cols) for i in range(cols)])

    def scattered(terms):
        parts = [[terms[k]] for k in range(chips)]
        for j in range(1, cores):
            for k in reversed(range(chips)):
                parts[k].append(swap_cores(terms[j * chips + k], j))
        return parts[0], [hop_chips(coded_sum(*parts[k]), k) for k in range(1, chips)]

    grads, both = packed(grad_center, grad_radius), packed(center, radius)
    held = [both] + [hop_chips(both, -k) for k in range(1, chips)]
    slots = {0: grads}
    for step in range(1, (rows + 1) // 2):
        slots[step] = lax.ppermute(slots[step - 1], "row", clockwise)
        slots[-step] = lax.ppermute(slots[1 - step], "row", counter)
        if step == 2:
            slots[step], weight = lax.optimization_barrier((slots[step], loaded(weight)))
    for j in range(1, cores):
        held += [swap_cores(value, -j) for value in held[:chips]]
    turned_c, turned_r = turned(held, 2)
    slots_c, slots_r = dict(slots), dict(slots)
    if rows % 2 == 0:
        step, count = rows // 2, grad_center.shape[0]
        slots_c[step] = lax.ppermute(slots[step - 1][:count], "row", clockwise)
        slots_r[-step] = lax.ppermute(slots[1 - step][count:], "row", counter)
    slots_c[0], turned_c, turned_r = lax.optimization_barrier((slots_c[0], turned_c, turned_r))

    terms_c, order_c = input_terms(
        rows, cols, tuple(slots_c), list(slots_c.values()), weight, False
    )
    near_c, far_c = scattered(terms_c)
    terms_r, order_r = input_terms(rows, cols, tuple(slots_r), list(slots_r.values()), weight, True)
    near_r, far_r = scattered(terms_r)
    through_center = center_terms(turned_c, order_c)
    weight_grad = weight_terms(through_center, turned_r, order_r, weight)
    return gated(near_c, far_c, active), gated(near_r, far_r, active), weight_grad


def solution(mesh):
    spec_in, spec_out, spec_weight = P("col", "row"), P("row", "col"), P("row", "col")
    return jax.shard_map(
        functools.partial(on_device, mesh.shape["row"], mesh.shape["col"]),
        mesh=mesh,
        in_specs=(spec_in, spec_in, spec_out, spec_out, spec_weight, spec_in),
        out_specs=(spec_in, spec_in, spec_weight),
        check_vma=False,
    )
```

```python
import functools

import jax
import jax.numpy as jnp
import numpy as np
from jax import lax
from jax.experimental import pallas as pl
from jax.experimental.pallas import tpu as pltpu
from jax.sharding import PartitionSpec as P

VMEM_LIMIT = 24 * 1024 * 1024
VMEM_MOST = 60 * 1024 * 1024
HERE = pl.BlockSpec(memory_space=pltpu.VMEM)
LANES = 128
LEVELS = np.float32(32000)
TINY = np.float32(2.0**-100)
ANYWHERE = pl.BlockSpec(memory_space=pl.ANY)
BY_LAST = (((1,), (1,)), ((), ()))
BY_TOKEN = (((1,), (0,)), ((), ()))
PAIR = 2


def ring_of(rows):
    return list(range(0, rows, PAIR)) + list(range(rows - 1, 0, -PAIR))


def on_ring(row, rows):
    return lax.select(lax.rem(row, PAIR) == 0, lax.div(row, PAIR), rows - 1 - lax.div(row, PAIR))


def off_ring(place, rows):
    return lax.select(place < rows // PAIR, PAIR * place, PAIR * (rows - place) - 1)


def apart(a, b, rows):
    ahead = lax.rem(a - b + rows, rows)
    return lax.min(ahead, rows - ahead)


def by_distance(rows):
    return [0] + [way * step for step in range(1, rows // 2) for way in (1, -1)] + [rows // 2]


def col_split(cols):
    return (cols // 2, 2) if cols % 2 == 0 else (cols, 1)


def spot(rows, cols, shift, all_near=False):
    chips, cores = col_split(cols)
    here, col = on_ring(lax.axis_index("row"), rows), lax.axis_index("col")
    x, my_core = lax.div(col, cores), lax.rem(col, cores)
    place = lax.rem(here + (rows - shift) % rows, rows)
    source = off_ring(place, rows)
    owner, half = lax.div(source, PAIR), lax.rem(source, PAIR)
    chip, core = lax.rem(lax.div(owner, cores) + chips - x, chips), lax.rem(owner, cores)
    near_core = lax.rem(core + cores - my_core, cores)
    far = abs(shift) > apart(here, rows - 1 - place, rows)
    piece = (near_core if all_near else lax.select(far | (chip == 0), near_core, core)) * chips + chip
    return piece, half, far


def shard_of(slot, half, held):
    first = half * held if slot.shape[0] > held else 0
    return slot[first : first + held, :]


def terms_of(lhs, weight, cores, own, others, kind):
    inner, chips = weight.shape[0], others[0].shape[1] + 1
    tile = min(256, inner)
    held = lhs.shape[0] // (cores * chips)
    rows = slice(kind * held, (kind + 1) * held)
    for i in range(inner // tile):
        span = slice(i * tile, (i + 1) * tile)
        block = weight[span, :]
        if kind:
            block = jnp.abs(block)
        terms = lax.dot_general(lhs, block, BY_LAST, preferred_element_type=jnp.float32)
        for n in range(cores * chips):
            core, chip = divmod(n, chips)
            part = terms[n * held : (n + 1) * held, :]
            if not chip:
                own[core][rows, span] = part
            elif len(others) == 1:
                others[0][core, chip - 1, rows, span] = part
            else:
                others[kind * cores + core][0, chip - 1, :, span] = part


def near_kernel(rows, cols, shifts, *refs):
    count = len(shifts)
    slots_c, slots_r, weight = refs[:count], refs[count : 2 * count], refs[2 * count]
    own, others, orders = refs[2 * count + 1 : -3], refs[-3:-2], refs[-2:]
    cores = len(own)
    middle = orders[0].shape[0] // 2
    held = middle // cols
    for n, shift in enumerate(shifts):
        piece, _, far = spot(rows, cols, shift)
        start = pl.multiple_of(lax.select(far, middle, 0) + piece * held, held)
        for half, (order, slots) in enumerate(zip(orders, (slots_c, slots_r))):
            order[pl.ds(start, held), :] = shard_of(slots[n], half, held)
    for kind, order in enumerate(orders):
        terms_of(order[:middle, :], weight, cores, own, others, kind)


def near_terms(rows, cols, held, shifts, slots_c, slots_r, weight):
    inner, width = weight.shape
    tokens = held * rows
    chips, cores = col_split(cols)
    found = pl.pallas_call(
        functools.partial(near_kernel, rows, cols, shifts),
        in_specs=[HERE] * (2 * len(shifts) + 1),
        out_specs=[HERE] * (cores + 3),
        out_shape=[jax.ShapeDtypeStruct((2 * held, inner), jnp.float32)] * cores
        + [jax.ShapeDtypeStruct((cores, chips - 1, 2 * held, inner), jnp.float32)]
        + [jax.ShapeDtypeStruct((tokens, width), jnp.bfloat16)] * 2,
        compiler_params=pltpu.CompilerParams(vmem_limit_bytes=VMEM_LIMIT),
    )(*slots_c, *slots_r, weight)
    return found[:-2], found[-2:]


def far_kernel(rows, cols, *refs):
    orders, lasts, (weight, *outs, work) = refs[:2], refs[2:4], refs[4:]
    cores = len(outs) // 3
    middle = work.shape[0]
    held = middle // cols
    piece, _, _ = spot(rows, cols, rows // 2, all_near=True)
    start = pl.multiple_of(piece * held, held)
    for half, (order, last) in enumerate(zip(orders, lasts)):
        work[...] = order[middle:, :]
        work[pl.ds(start, held), :] = last[...]
        terms_of(work[...], weight, cores, outs[:cores], outs[cores:], half)


def far_terms(rows, cols, orders, lasts, weight):
    inner, width = weight.shape
    held = lasts[0].shape[0]
    tokens = held * rows
    chips, cores = col_split(cols)
    return pl.pallas_call(
        functools.partial(far_kernel, rows, cols),
        in_specs=[HERE] * 5,
        out_specs=[HERE] * (3 * cores),
        out_shape=[jax.ShapeDtypeStruct((2 * held, inner), jnp.float32)] * cores
        + [jax.ShapeDtypeStruct((1, chips - 1, held, inner), jnp.float32)] * (2 * cores),
        scratch_shapes=[pltpu.VMEM((tokens // 2, width), jnp.bfloat16)],
        compiler_params=pltpu.CompilerParams(vmem_limit_bytes=VMEM_LIMIT),
    )(*orders, *lasts, weight)


def sum_kernel(chips, *refs):
    terms, outs = refs[: 1 - chips], refs[1 - chips :]
    rows, width = outs[0].shape[0] // 2, outs[0].shape[1] - LANES
    for k, out in enumerate(outs):
        for kind in range(2):
            mine = slice(kind * rows, (kind + 1) * rows)
            if len(terms) == 1:
                parts = [terms[0][j, k, mine, :] for j in range(terms[0].shape[0])]
            else:
                count = len(terms) // 2
                parts = [ref[0, k] for ref in terms[kind * count : (kind + 1) * count]]
            total = parts[0]
            for part in parts[1:]:
                total = total + part
            most = jnp.max(jnp.abs(total), axis=1, keepdims=True)
            exponent = jnp.ceil(jnp.log2(jnp.maximum(most, TINY)) + 1e-3)
            coded = jnp.round(total * (LEVELS / jnp.exp2(exponent)))
            out[mine, :width] = coded.astype(jnp.int16)
            out[mine, width:] = jnp.broadcast_to(exponent, (rows, LANES)).astype(jnp.int16)


def coded_sums(chips, rows, terms):
    width = terms[0].shape[3]
    return pl.pallas_call(
        functools.partial(sum_kernel, chips),
        in_specs=[HERE] * len(terms),
        out_specs=[HERE] * (chips - 1),
        out_shape=[jax.ShapeDtypeStruct((rows, width + LANES), jnp.int16)] * (chips - 1),
        compiler_params=pltpu.CompilerParams(vmem_limit_bytes=VMEM_LIMIT),
    )(*terms)


def gate_kernel(rows, cols, near, far, *refs):
    rounds, (active, *outs) = refs[:-3], refs[-3:]
    rounds = rounds[: near + far], rounds[near + far :]
    held = active.shape[0] // PAIR
    width = active.shape[1]
    here, col = on_ring(lax.axis_index("row"), rows), lax.axis_index("col")
    first = apart(here, on_ring(PAIR * col, rows), rows)
    second = apart(here, on_ring(PAIR * col + 1, rows), rows)
    halves = lax.select(first < second, 0, 1), lax.select(first < second, 1, 0)
    for half, parts in zip(halves, rounds):
        span = pl.ds(pl.multiple_of(half * held, held), held)
        gate = active[span, :].astype(jnp.float32)
        for n, out in enumerate(outs):
            mine = slice(n * held, (n + 1) * held)
            total = parts[0][mine, :]
            for part in parts[1:near]:
                total = total + part[mine, :]
            for part in parts[near:]:
                exponent = part[mine, width : width + 1].astype(jnp.float32)
                total = total + part[mine, :width].astype(jnp.float32) * (
                    jnp.exp2(exponent) / LEVELS
                )
            out[span, :] = gate * total


def gated(rows, cols, rounds, active):
    near, far = rounds[0]
    parts = [part for found in rounds for kind in found for part in kind]
    size = active.size
    return pl.pallas_call(
        functools.partial(gate_kernel, rows, cols, len(near), len(far)),
        in_specs=[HERE] * (len(parts) + 1),
        out_specs=[HERE] * 2,
        out_shape=[jax.ShapeDtypeStruct(active.shape, jnp.float32)] * 2,
        compiler_params=pltpu.CompilerParams(vmem_limit_bytes=VMEM_LIMIT),
    )(*parts, active)


def pack_kernel(first, second, out, both, sems):
    rows = first.shape[0]
    spans = [pl.ds(0, rows), pl.ds(rows, rows)]
    copies = [
        pltpu.make_async_copy(source, both.at[span, :], sem)
        for source, span, sem in zip((first, second), spans, (sems.at[0], sems.at[1]))
    ]
    onward = [
        pltpu.make_async_copy(both.at[span, :], out.at[span, :], sem)
        for span, sem in zip(spans, (sems.at[2], sems.at[3]))
    ]
    for copy in copies:
        copy.start()
    for copy, then in zip(copies, onward):
        copy.wait()
        then.start()
    for then in onward:
        then.wait()


def packed(first, second):
    rows, width = first.shape
    return pl.pallas_call(
        pack_kernel,
        in_specs=[ANYWHERE] * 2,
        out_specs=ANYWHERE,
        out_shape=jax.ShapeDtypeStruct((2 * rows, width), first.dtype),
        scratch_shapes=[pltpu.VMEM((2 * rows, width), first.dtype), pltpu.SemaphoreType.DMA((4,))],
        compiler_params=pltpu.CompilerParams(vmem_limit_bytes=VMEM_MOST),
    )(first, second)


def stack_kernel(*refs):
    *parts, out = refs
    rows = parts[0].shape[0]
    for n, part in enumerate(parts):
        out[n * rows : (n + 1) * rows, :] = part[...]


def stacked(parts):
    rows, width = parts[0].shape
    return pl.pallas_call(
        stack_kernel,
        in_specs=[HERE] * len(parts),
        out_specs=HERE,
        out_shape=jax.ShapeDtypeStruct((len(parts) * rows, width), parts[0].dtype),
        compiler_params=pltpu.CompilerParams(vmem_limit_bytes=VMEM_LIMIT),
    )(*parts)


def turn_kernel(rows, cols, *refs):
    held, outs, whole, order = refs[:-6], refs[-6:-2], refs[-2], refs[-1]
    chips = cols // len(held)
    owned = whole.shape[0] // cols
    shard = owned // PAIR
    near = outs[0].shape[1]
    for kind in range(2):
        for n in range(cols):
            first = (2 * (n % chips) + kind) * owned
            whole[n * owned : (n + 1) * owned, :] = held[n // chips][first : first + owned, :]
        for n, shift in enumerate(by_distance(rows)):
            piece, half, _ = spot(rows, cols, shift, all_near=True)
            start = pl.multiple_of((piece * PAIR + half) * shard, shard)
            order[n * shard : (n + 1) * shard, :] = whole[pl.ds(start, shard), :]
        outs[kind][...] = order[:near, :].T
        outs[2 + kind][...] = order[near:, :].T


def turned(rows, cols, held):
    both, inner = held[0].shape
    tokens = both // 2 * len(held)
    return pl.pallas_call(
        functools.partial(turn_kernel, rows, cols),
        in_specs=[HERE] * len(held),
        out_specs=[HERE] * 4,
        out_shape=[jax.ShapeDtypeStruct((inner, tokens // 2), jnp.bfloat16)] * 4,
        scratch_shapes=[pltpu.VMEM((tokens, inner), jnp.bfloat16)] * 2,
        compiler_params=pltpu.CompilerParams(vmem_limit_bytes=VMEM_LIMIT),
    )(*held)


def gather_slots(slots_c, slots_r, grads):
    held = grads[0].shape[0] // len(slots_c)
    for half, (grad, slots) in enumerate(zip(grads, (slots_c, slots_r))):
        for n, slot in enumerate(slots):
            grad[n * held : (n + 1) * held, :] = shard_of(slot, half, held)


def weight_part(inputs, grads, weight, span):
    through_center, through_radius = (
        lax.dot_general(ref[span, :], grad[...], BY_TOKEN, preferred_element_type=jnp.float32)
        for ref, grad in zip(inputs, grads)
    )
    w = weight[span, :].astype(jnp.float32)
    signed = jnp.where(w > 0, through_radius, jnp.where(w < 0, -through_radius, 0.0))
    return through_center + signed


def first_kernel(count, *refs):
    inputs, slots_c, slots_r = refs[:2], refs[2 : 2 + count], refs[2 + count : 2 + 2 * count]
    weight, out, *grads = refs[2 + 2 * count :]
    gather_slots(slots_c, slots_r, grads)
    tile = min(256, out.shape[0])
    for n in range(out.shape[0] // tile):
        span = slice(n * tile, (n + 1) * tile)
        out[span, :] = weight_part(inputs, grads, weight, span)


def first_weight_terms(inputs, slots_c, slots_r, weight):
    inner, width = weight.shape
    tokens = inputs[0].shape[1]
    return pl.pallas_call(
        functools.partial(first_kernel, len(slots_c)),
        in_specs=[HERE] * (3 + 2 * len(slots_c)),
        out_specs=HERE,
        out_shape=jax.ShapeDtypeStruct((inner, width), jnp.float32),
        scratch_shapes=[pltpu.VMEM((tokens, width), jnp.bfloat16)] * 2,
        compiler_params=pltpu.CompilerParams(vmem_limit_bytes=VMEM_LIMIT),
    )(*inputs, *slots_c, *slots_r, weight)


def weight_kernel(count, scale, begun, *refs):
    inputs, slots_c, slots_r = refs[:2], refs[2 : 2 + count], refs[2 + count : 2 + 2 * count]
    weight, out, grad_c, grad_r, parts, sems = refs[2 + 2 * count :]
    gather_slots(slots_c, slots_r, (grad_c, grad_r))
    tile = parts.shape[1]
    copies = []
    for n in range(out.shape[0] // tile):
        span = slice(n * tile, (n + 1) * tile)
        part, sem = parts.at[n % 2], sems.at[n % 2]
        if n >= 2:
            copies[n - 2].wait()
        part[...] = (begun[span, :] + weight_part(inputs, (grad_c, grad_r), weight, span)) * scale
        copies.append(pltpu.make_async_copy(part, out.at[pl.ds(n * tile, tile), :], sem))
        copies[n].start()
    for copy in copies[-2:]:
        copy.wait()


def weight_terms(begun, inputs, slots_c, slots_r, weight):
    inner, width = weight.shape
    tokens = inputs[0].shape[1]
    tile = min(256, inner)
    scale = np.float32(1.0) / np.sqrt(np.float32(2 * tokens))
    return pl.pallas_call(
        functools.partial(weight_kernel, len(slots_c), scale),
        in_specs=[HERE] * (4 + 2 * len(slots_c)),
        out_specs=ANYWHERE,
        out_shape=jax.ShapeDtypeStruct((inner, width), jnp.float32),
        scratch_shapes=[pltpu.VMEM((tokens, width), jnp.bfloat16)] * 2
        + [pltpu.VMEM((2, tile, width), jnp.float32), pltpu.SemaphoreType.DMA((2,))],
        compiler_params=pltpu.CompilerParams(vmem_limit_bytes=VMEM_LIMIT),
    )(begun, *inputs, *slots_c, *slots_r, weight)


def on_device(rows, cols, center, radius, grad_center, grad_radius, weight, active):
    chips, cores = col_split(cols)
    held = grad_center.shape[0]
    assert rows % 2 == 0 and center.shape[0] == PAIR * held
    ring = ring_of(rows)
    clockwise = [(ring[i], ring[(i + 1) % rows]) for i in range(rows)]
    counter = [(b, a) for a, b in clockwise]
    last = rows // 2

    def swap_cores(value, j):
        perm = [(i, i - i % cores + (i % cores + j) % cores) for i in range(cols)]
        return lax.ppermute(value, "col", perm)

    def hop_chips(value, k):
        return lax.ppermute(value, "col", [(i, (i + k * cores) % cols) for i in range(cols)])

    def summed(own, others, *done):
        if len(others) == 1:
            groups = [[k * cores + j for j in range(cores)] for k in range(chips)]
            parts = [lax.all_to_all(others[0], "col", 0, 0, axis_index_groups=groups, tiled=True)]
        else:
            parts = [swap_cores(part, n % cores) if n % cores else part for n, part in enumerate(others)]
        if done:
            parts, _ = lax.optimization_barrier((parts, done))
        own = [own[0]] + [swap_cores(own[j], j) for j in range(1, cores)]
        return own, coded_sums(chips, 2 * held, parts)

    def hopped(coded):
        return [hop_chips(value, k + 1) for k, value in enumerate(coded)]

    both = packed(center, radius)
    inputs = [both] + [hop_chips(both, -k) for k in range(1, chips)]
    slots_c, slots_r = {0: grad_center}, {0: grad_radius}
    shifts = by_distance(rows)
    first = shifts[:last]
    for step in range(1, last):
        if step == 3:
            heads = slots_c[2], slots_c[-2], slots_r[2], slots_r[-2]
            heads = lax.optimization_barrier(heads)
            slots_c[2], slots_c[-2], slots_r[2], slots_r[-2] = heads
            inputs, _ = lax.optimization_barrier((inputs, heads[0]))
            inputs = [stacked(inputs)]
            inputs += [swap_cores(inputs[0], -j) for j in range(1, cores)]
        for slots in (slots_c, slots_r):
            slots[step] = lax.ppermute(slots[step - 1], "row", clockwise)
            slots[-step] = lax.ppermute(slots[1 - step], "row", counter)
    nearer_c, nearer_r, further_c, further_r = turned(rows, cols, inputs)
    begun = first_weight_terms(
        (nearer_c, nearer_r), [slots_c[s] for s in first], [slots_r[s] for s in first], weight
    )
    slots_c[last - 1], begun = lax.optimization_barrier((slots_c[last - 1], begun))

    lasts = (
        lax.ppermute(slots_c[last - 1], "row", clockwise),
        lax.ppermute(slots_r[1 - last], "row", counter),
    )
    found = shifts[:-1]
    terms, orders = near_terms(
        rows, cols, held, found, [slots_c[s] for s in found], [slots_r[s] for s in found], weight
    )
    near_0, coded_0 = summed(terms[:-1], terms[-1:])
    lasts, coded_0 = lax.optimization_barrier((lasts, coded_0))
    far_0 = hopped(coded_0)
    terms = far_terms(rows, cols, orders, lasts, weight)
    near_1, coded_1 = summed(terms[:cores], terms[cores:], *far_0)
    far_1 = hopped(coded_1)
    rest = shifts[last:-1]
    weight_grad = weight_terms(
        begun,
        (further_c, further_r),
        [slots_c[s] for s in rest] + [lasts[0]],
        [slots_r[s] for s in rest] + [lasts[1]],
        weight,
    )
    return *gated(rows, cols, ((near_0, far_0), (near_1, far_1)), active), weight_grad


def solution(mesh):
    spec_in, spec_out, spec_weight = P("col", "row"), P("row", "col"), P("row", "col")
    return jax.shard_map(
        functools.partial(on_device, mesh.shape["row"], mesh.shape["col"]),
        mesh=mesh,
        in_specs=(spec_in, spec_in, spec_out, spec_out, spec_weight, spec_in),
        out_specs=(spec_in, spec_in, spec_weight),
        check_vma=False,
    )
```

```python
import functools

import jax
import jax.numpy as jnp
import numpy as np
from jax import lax
from jax.experimental import pallas as pl
from jax.experimental.pallas import tpu as pltpu
from jax.sharding import PartitionSpec as P

VMEM_LIMIT = 24 * 1024 * 1024
VMEM_MOST = 60 * 1024 * 1024
HERE = pl.BlockSpec(memory_space=pltpu.VMEM)
LANES = 128
LEVELS = np.float32(32000)
TINY = np.float32(2.0**-100)
ANYWHERE = pl.BlockSpec(memory_space=pl.ANY)
BY_LAST = (((1,), (1,)), ((), ()))
BY_TOKEN = (((1,), (0,)), ((), ()))
PAIR = 2


def ring_of(rows):
    return list(range(0, rows, PAIR)) + list(range(rows - 1, 0, -PAIR))


def on_ring(row, rows):
    return lax.select(lax.rem(row, PAIR) == 0, lax.div(row, PAIR), rows - 1 - lax.div(row, PAIR))


def off_ring(place, rows):
    return lax.select(place < rows // PAIR, PAIR * place, PAIR * (rows - place) - 1)


def apart(a, b, rows):
    ahead = lax.rem(a - b + rows, rows)
    return lax.min(ahead, rows - ahead)


def by_distance(rows):
    return [0] + [way * step for step in range(1, rows // 2) for way in (1, -1)] + [rows // 2]


def col_split(cols):
    return (cols // 2, 2) if cols % 2 == 0 else (cols, 1)


def spot(rows, cols, shift):
    chips, cores = col_split(cols)
    here, col = on_ring(lax.axis_index("row"), rows), lax.axis_index("col")
    x, core = lax.div(col, cores), lax.rem(col, cores)
    place = lax.rem(here + (rows - shift) % rows, rows)
    source = off_ring(place, rows)
    owner, half = lax.div(source, PAIR), lax.rem(source, PAIR)
    away = lax.rem(lax.rem(owner, cores) + cores - core, cores)
    piece = away * chips + lax.rem(lax.div(owner, cores) + chips - x, chips)
    return piece, half, abs(shift) > apart(here, rows - 1 - place, rows)


def row_of(rows, cols, shift, held):
    piece, _, far = spot(rows, cols, shift)
    return pl.multiple_of((lax.select(far, cols, 0) + piece) * held, held)


def terms_of(lhs, weight, outs, kind):
    cores, chips = len(outs) // 2, outs[-1].shape[0] + 1
    inner = weight.shape[0]
    tile = min(256, inner)
    held = lhs.shape[0] // (cores * chips)
    rows = slice(kind * held, (kind + 1) * held)
    for i in range(inner // tile):
        span = slice(i * tile, (i + 1) * tile)
        terms = lax.dot_general(
            lhs, weight[span, :], BY_LAST, preferred_element_type=jnp.float32
        )
        for n in range(cores * chips):
            core, chip = divmod(n, chips)
            part = terms[n * held : (n + 1) * held, :]
            if chip:
                outs[cores + core][chip - 1, rows, span] = part
            else:
                outs[core][rows, span] = part


def terms_shapes(cols, held, inner):
    chips, cores = col_split(cols)
    return [jax.ShapeDtypeStruct((2 * held, inner), jnp.float32)] * cores + [
        jax.ShapeDtypeStruct((chips - 1, 2 * held, inner), jnp.float32)
    ] * cores


def near_kernel(rows, cols, shifts, *refs):
    count = len(shifts)
    slots, weights, outs, orders = refs[: 2 * count], refs[2 * count : 2 * count + 2], refs[2 * count + 2 : -2], refs[-2:]
    held = slots[0].shape[0]
    for n, shift in enumerate(shifts):
        start = row_of(rows, cols, shift, held)
        for kind, order in enumerate(orders):
            order[pl.ds(start, held), :] = slots[kind * count + n][...]
    for kind, (order, weight) in enumerate(zip(orders, weights)):
        terms_of(order[: cols * held, :], weight, outs, kind)


def near_terms(rows, cols, shifts, slots_c, slots_r, weights):
    inner, width = weights[0].shape
    held = slots_c[0].shape[0]
    shapes = terms_shapes(cols, held, inner)
    found = pl.pallas_call(
        functools.partial(near_kernel, rows, cols, shifts),
        in_specs=[HERE] * (2 * len(shifts) + 2),
        out_specs=[HERE] * (len(shapes) + 2),
        out_shape=shapes + [jax.ShapeDtypeStruct((held * rows, width), jnp.bfloat16)] * 2,
        compiler_params=pltpu.CompilerParams(vmem_limit_bytes=VMEM_LIMIT),
    )(*slots_c, *slots_r, *weights)
    return found[:-2], found[-2:]


def far_kernel(rows, cols, *refs):
    lasts, weights, outs, orders = refs[2:4], refs[4:6], refs[6:-2], refs[-2:]
    held = lasts[0].shape[0]
    start = row_of(rows, cols, rows // 2, held)
    for kind, (order, last, weight) in enumerate(zip(orders, lasts, weights)):
        order[pl.ds(start, held), :] = last[...]
        terms_of(order[cols * held :, :], weight, outs, kind)


def far_terms(rows, cols, orders, lasts, weights):
    shapes = terms_shapes(cols, lasts[0].shape[0], weights[0].shape[0])
    found = pl.pallas_call(
        functools.partial(far_kernel, rows, cols),
        in_specs=[HERE] * 6,
        out_specs=[HERE] * (len(shapes) + 2),
        out_shape=shapes + [jax.ShapeDtypeStruct(order.shape, order.dtype) for order in orders],
        input_output_aliases={0: len(shapes), 1: len(shapes) + 1},
        compiler_params=pltpu.CompilerParams(vmem_limit_bytes=VMEM_LIMIT),
    )(*orders, *lasts, *weights)
    return found[:-2], found[-2:]


def sum_kernel(count, *refs):
    parts, outs = refs[:count], refs[count:]
    rows, width = parts[0].shape[1:]
    for k, out in enumerate(outs):
        total = parts[0][k]
        for part in parts[1:]:
            total = total + part[k]
        most = jnp.max(jnp.abs(total), axis=1, keepdims=True)
        exponent = jnp.ceil(jnp.log2(jnp.maximum(most, TINY)) + 1e-3)
        coded = jnp.round(total * (LEVELS / jnp.exp2(exponent)))
        out[:, :width] = coded.astype(jnp.int16)
        out[:, width:] = jnp.broadcast_to(exponent, (rows, LANES)).astype(jnp.int16)


def coded_sums(parts):
    others, rows, width = parts[0].shape
    return pl.pallas_call(
        functools.partial(sum_kernel, len(parts)),
        in_specs=[HERE] * len(parts),
        out_specs=[HERE] * others,
        out_shape=[jax.ShapeDtypeStruct((rows, width + LANES), jnp.int16)] * others,
        compiler_params=pltpu.CompilerParams(vmem_limit_bytes=VMEM_LIMIT),
    )(*parts)


def gate_kernel(rows, cols, near, far, *refs):
    rounds, (active, *outs) = refs[:-3], refs[-3:]
    rounds = rounds[: near + far], rounds[near + far :]
    held = active.shape[0] // PAIR
    width = active.shape[1]
    here, col = on_ring(lax.axis_index("row"), rows), lax.axis_index("col")
    first = apart(here, on_ring(PAIR * col, rows), rows)
    second = apart(here, on_ring(PAIR * col + 1, rows), rows)
    halves = lax.select(first < second, 0, 1), lax.select(first < second, 1, 0)
    for half, parts in zip(halves, rounds):
        span = pl.ds(pl.multiple_of(half * held, held), held)
        gate = active[span, :].astype(jnp.float32)
        for n, out in enumerate(outs):
            mine = slice(n * held, (n + 1) * held)
            total = parts[0][mine, :]
            for part in parts[1:near]:
                total = total + part[mine, :]
            for part in parts[near:]:
                exponent = part[mine, width : width + 1].astype(jnp.float32)
                total = total + part[mine, :width].astype(jnp.float32) * (
                    jnp.exp2(exponent) / LEVELS
                )
            out[span, :] = gate * total


def gated(rows, cols, rounds, active):
    near, far = rounds[0]
    parts = [part for found in rounds for kind in found for part in kind]
    size = active.size
    return pl.pallas_call(
        functools.partial(gate_kernel, rows, cols, len(near), len(far)),
        in_specs=[HERE] * (len(parts) + 1),
        out_specs=[HERE] * 2,
        out_shape=[jax.ShapeDtypeStruct(active.shape, jnp.float32)] * 2,
        compiler_params=pltpu.CompilerParams(vmem_limit_bytes=VMEM_LIMIT),
    )(*parts, active)


def parts_kernel(weight, *refs):
    magnitude, sign = refs[-2:]
    tile = min(256, weight.shape[0])
    for start in range(0, weight.shape[0], tile):
        span = slice(start, start + tile)
        w = weight[span, :].astype(jnp.float32)
        magnitude[span, :] = jnp.abs(w).astype(jnp.bfloat16)
        sign[span, :] = jnp.where(w > 0, 1.0, jnp.where(w < 0, -1.0, 0.0)).astype(jnp.bfloat16)


def parts_of(weight, *held):
    return pl.pallas_call(
        parts_kernel,
        in_specs=[HERE] * (1 + len(held)),
        out_specs=[HERE] * 2,
        out_shape=[jax.ShapeDtypeStruct(weight.shape, weight.dtype)] * 2,
        compiler_params=pltpu.CompilerParams(vmem_limit_bytes=VMEM_LIMIT),
    )(weight, *held)


def pack_kernel(first, second, out, both, sems):
    rows = first.shape[0]
    spans = [pl.ds(0, rows), pl.ds(rows, rows)]
    copies = [
        pltpu.make_async_copy(source, both.at[span, :], sem)
        for source, span, sem in zip((first, second), spans, (sems.at[0], sems.at[1]))
    ]
    onward = [
        pltpu.make_async_copy(both.at[span, :], out.at[span, :], sem)
        for span, sem in zip(spans, (sems.at[2], sems.at[3]))
    ]
    for copy in copies:
        copy.start()
    for copy, then in zip(copies, onward):
        copy.wait()
        then.start()
    for then in onward:
        then.wait()


def packed(first, second):
    rows, width = first.shape
    return pl.pallas_call(
        pack_kernel,
        in_specs=[ANYWHERE] * 2,
        out_specs=ANYWHERE,
        out_shape=jax.ShapeDtypeStruct((2 * rows, width), first.dtype),
        scratch_shapes=[pltpu.VMEM((2 * rows, width), first.dtype), pltpu.SemaphoreType.DMA((4,))],
        compiler_params=pltpu.CompilerParams(vmem_limit_bytes=VMEM_MOST),
    )(first, second)


def pack_kernel(first, second, out, both, sems):
    rows = first.shape[0]
    spans = [pl.ds(0, rows), pl.ds(rows, rows)]
    copies = [
        pltpu.make_async_copy(source, both.at[span, :], sem)
        for source, span, sem in zip((first, second), spans, (sems.at[0], sems.at[1]))
    ]
    onward = [
        pltpu.make_async_copy(both.at[span, :], out.at[span, :], sem)
        for span, sem in zip(spans, (sems.at[2], sems.at[3]))
    ]
    for copy in copies:
        copy.start()
    for copy, then in zip(copies, onward):
        copy.wait()
        then.start()
    for then in onward:
        then.wait()


def packed(first, second):
    rows, width = first.shape
    return pl.pallas_call(
        pack_kernel,
        in_specs=[ANYWHERE] * 2,
        out_specs=ANYWHERE,
        out_shape=jax.ShapeDtypeStruct((2 * rows, width), first.dtype),
        scratch_shapes=[pltpu.VMEM((2 * rows, width), first.dtype), pltpu.SemaphoreType.DMA((4,))],
        compiler_params=pltpu.CompilerParams(vmem_limit_bytes=VMEM_MOST),
    )(first, second)


def stack_kernel(*refs):
    *parts, out = refs
    rows = parts[0].shape[0]
    for n, part in enumerate(parts):
        out[n * rows : (n + 1) * rows, :] = part[...]


def stacked(parts):
    rows, width = parts[0].shape
    return pl.pallas_call(
        stack_kernel,
        in_specs=[HERE] * len(parts),
        out_specs=HERE,
        out_shape=jax.ShapeDtypeStruct((len(parts) * rows, width), parts[0].dtype),
        compiler_params=pltpu.CompilerParams(vmem_limit_bytes=VMEM_LIMIT),
    )(*parts)


def turn_kernel(rows, cols, *refs):
    held, outs, whole, order = refs[:cols], refs[cols:-2], refs[-2], refs[-1]
    owned = whole.shape[0] // cols
    shard = owned // PAIR
    for kind, out in enumerate(outs):
        for n, ref in enumerate(held):
            whole[n * owned : (n + 1) * owned, :] = ref[kind * owned : (kind + 1) * owned, :]
        for shift in by_distance(rows):
            piece, half, _ = spot(rows, cols, shift)
            start = pl.multiple_of((piece * PAIR + half) * shard, shard)
            to = row_of(rows, cols, shift, shard)
            order[pl.ds(to, shard), :] = whole[pl.ds(start, shard), :]
        out[...] = order[...].T


def turned(rows, cols, held):
    both, inner = held[0].shape
    tokens = both // 2 * cols
    return pl.pallas_call(
        functools.partial(turn_kernel, rows, cols),
        in_specs=[HERE] * cols,
        out_specs=[HERE] * 2,
        out_shape=[jax.ShapeDtypeStruct((inner, tokens), jnp.bfloat16)] * 2,
        scratch_shapes=[pltpu.VMEM((tokens, inner), jnp.bfloat16)] * 2,
        compiler_params=pltpu.CompilerParams(vmem_limit_bytes=VMEM_LIMIT),
    )(*held)


def weight_kernel(scale, center, radius, grad_c, grad_r, sign, out, parts, sems):
    tile = parts.shape[2]
    copies = []
    for n in range(out.shape[1] // tile):
        span = slice(n * tile, (n + 1) * tile)
        part, sem = parts.at[n % 2], sems.at[n % 2]
        if n >= 2:
            copies[n - 2].wait()
        through_center, through_radius = (
            lax.dot_general(ref[...], grad[:, span], BY_TOKEN, preferred_element_type=jnp.float32)
            for ref, grad in ((center, grad_c), (radius, grad_r))
        )
        signed = sign[:, span].astype(jnp.float32) * through_radius
        part[...] = (through_center + signed) * scale
        copies.append(pltpu.make_async_copy(part, out.at[:, pl.ds(n * tile, tile)], sem))
        copies[n].start()
    for copy in copies[-2:]:
        copy.wait()


def weight_terms(inputs, grads, sign):
    inner, width = sign.shape
    tile = min(256, width)
    scale = np.float32(1.0) / np.sqrt(np.float32(grads[0].shape[0]))
    return pl.pallas_call(
        functools.partial(weight_kernel, scale),
        in_specs=[HERE] * 5,
        out_specs=ANYWHERE,
        out_shape=jax.ShapeDtypeStruct((inner, width), jnp.float32),
        scratch_shapes=[pltpu.VMEM((2, inner, tile), jnp.float32), pltpu.SemaphoreType.DMA((2,))],
        compiler_params=pltpu.CompilerParams(vmem_limit_bytes=VMEM_LIMIT),
    )(*inputs, *grads, sign)


def on_device(rows, cols, center, radius, grad_center, grad_radius, weight, active):
    chips, cores = col_split(cols)
    held = grad_center.shape[0]
    assert rows % 2 == 0 and center.shape[0] == PAIR * held
    ring = ring_of(rows)
    clockwise = [(ring[i], ring[(i + 1) % rows]) for i in range(rows)]
    counter = [(b, a) for a, b in clockwise]
    last = rows // 2

    def swap_cores(value, j):
        perm = [(i, i - i % cores + (i % cores + j) % cores) for i in range(cols)]
        return lax.ppermute(value, "col", perm)

    def hop_chips(value, k):
        return lax.ppermute(value, "col", [(i, (i + k * cores) % cols) for i in range(cols)])

    def summed(terms):
        own, others = ([found[0]] + [swap_cores(found[j], j) for j in range(1, cores)]
                       for found in (terms[:cores], terms[cores:]))
        return own, [hop_chips(value, k + 1) for k, value in enumerate(coded_sums(others))]

    both = packed(center, radius)
    inputs = [both] + [hop_chips(both, -k) for k in range(1, chips)]
    slots_c, slots_r = {0: grad_center}, {0: grad_radius}
    shifts = by_distance(rows)
    for step in range(1, last):
        for slots in (slots_c, slots_r):
            slots[step] = lax.ppermute(slots[step - 1], "row", clockwise)
            slots[-step] = lax.ppermute(slots[1 - step], "row", counter)
    magnitude, sign = parts_of(weight, grad_center, grad_radius)
    weights = weight, magnitude
    slots_r[1 - last], weights = lax.optimization_barrier((slots_r[1 - last], weights))
    lasts = (
        lax.ppermute(slots_c[last - 1], "row", clockwise),
        lax.ppermute(slots_r[1 - last], "row", counter),
    )
    found = shifts[:-1]
    slots_c[0], inputs = lax.optimization_barrier((slots_c[0], inputs))
    terms, orders = near_terms(
        rows, cols, found, [slots_c[s] for s in found], [slots_r[s] for s in found], weights
    )
    near = summed(terms)
    terms, orders = far_terms(rows, cols, orders, lasts, weights)
    far = summed(terms)
    inputs, _ = lax.optimization_barrier((inputs, orders))
    for j in range(1, cores):
        inputs += [swap_cores(value, -j) for value in inputs[:chips]]
    weight_grad = weight_terms(turned(rows, cols, inputs), orders, sign)
    return *gated(rows, cols, (near, far), active), weight_grad


def solution(mesh):
    spec_in, spec_out, spec_weight = P("col", "row"), P("row", "col"), P("row", "col")
    return jax.shard_map(
        functools.partial(on_device, mesh.shape["row"], mesh.shape["col"]),
        mesh=mesh,
        in_specs=(spec_in, spec_in, spec_out, spec_out, spec_weight, spec_in),
        out_specs=(spec_in, spec_in, spec_weight),
        check_vma=False,
    )
```

```python
import functools

import jax
import jax.numpy as jnp
import numpy as np
from jax import lax
from jax.experimental import pallas as pl
from jax.experimental.pallas import tpu as pltpu
from jax.sharding import PartitionSpec as P

VMEM_LIMIT = 24 * 1024 * 1024
VMEM_MOST = 60 * 1024 * 1024
HERE = pl.BlockSpec(memory_space=pltpu.VMEM)
LANES = 128
BITS, LOWEST = 8, 100
LEVELS = np.float32(32000)
TINY = np.float32(2.0**-100)
ANYWHERE = pl.BlockSpec(memory_space=pl.ANY)
BY_LAST = (((1,), (1,)), ((), ()))
BY_TOKEN = (((1,), (0,)), ((), ()))
PAIR = 2


def ring_of(rows):
    return list(range(0, rows, PAIR)) + list(range(rows - 1, 0, -PAIR))


def on_ring(row, rows):
    return lax.select(lax.rem(row, PAIR) == 0, lax.div(row, PAIR), rows - 1 - lax.div(row, PAIR))


def off_ring(place, rows):
    return lax.select(place < rows // PAIR, PAIR * place, PAIR * (rows - place) - 1)


def apart(a, b, rows):
    ahead = lax.rem(a - b + rows, rows)
    return lax.min(ahead, rows - ahead)


def by_distance(rows):
    return [0] + [way * step for step in range(1, rows // 2) for way in (1, -1)] + [rows // 2]


def col_split(cols):
    return (cols // 2, 2) if cols % 2 == 0 else (cols, 1)


def spot(rows, cols, shift):
    chips, cores = col_split(cols)
    here, col = on_ring(lax.axis_index("row"), rows), lax.axis_index("col")
    x, core = lax.div(col, cores), lax.rem(col, cores)
    place = lax.rem(here + (rows - shift) % rows, rows)
    source = off_ring(place, rows)
    owner, half = lax.div(source, PAIR), lax.rem(source, PAIR)
    away = lax.rem(lax.rem(owner, cores) + cores - core, cores)
    piece = away * chips + lax.rem(lax.div(owner, cores) + chips - x, chips)
    return piece, half, abs(shift) > apart(here, rows - 1 - place, rows)


def row_of(rows, cols, shift, held):
    piece, _, far = spot(rows, cols, shift)
    return pl.multiple_of((lax.select(far, cols, 0) + piece) * held, held)


def terms_of(lhs, weight, outs, kind):
    cores, chips = len(outs) // 2, outs[-1].shape[0] + 1
    inner = weight.shape[0]
    tile = min(256, inner)
    held = lhs.shape[0] // (cores * chips)
    rows = slice(kind * held, (kind + 1) * held)
    for i in range(inner // tile):
        span = slice(i * tile, (i + 1) * tile)
        terms = lax.dot_general(
            lhs, weight[span, :], BY_LAST, preferred_element_type=jnp.float32
        )
        for n in range(cores * chips):
            core, chip = divmod(n, chips)
            part = terms[n * held : (n + 1) * held, :]
            if chip:
                outs[cores + core][chip - 1, rows, span] = part
            else:
                outs[core][rows, span] = part


def terms_shapes(cols, held, inner):
    chips, cores = col_split(cols)
    return [jax.ShapeDtypeStruct((2 * held, inner), jnp.float32)] * cores + [
        jax.ShapeDtypeStruct((chips - 1, 2 * held, inner), jnp.float32)
    ] * cores


def near_kernel(rows, cols, shifts, kind, *refs):
    count = len(shifts)
    slots, weight, outs, order = refs[:count], refs[count], refs[-1 - 2 * col_split(cols)[1] : -1], refs[-1]
    held = slots[0].shape[0]
    for shift, slot in zip(shifts, slots):
        order[pl.ds(row_of(rows, cols, shift, held), held), :] = slot[...]
    terms_of(order[: cols * held, :], weight, outs, kind)


def near_terms(rows, cols, shifts, slots, weight, kind, begun=()):
    inner, width = weight.shape
    held = slots[0].shape[0]
    shapes = terms_shapes(cols, held, inner)
    found = pl.pallas_call(
        functools.partial(near_kernel, rows, cols, shifts, kind),
        in_specs=[HERE] * (len(slots) + 1 + len(begun)),
        out_specs=[HERE] * (len(shapes) + 1),
        out_shape=shapes + [jax.ShapeDtypeStruct((held * rows, width), jnp.bfloat16)],
        input_output_aliases={len(slots) + 1 + n: n for n in range(len(begun))},
        compiler_params=pltpu.CompilerParams(vmem_limit_bytes=VMEM_LIMIT),
    )(*slots, weight, *begun)
    return found[:-1], found[-1]


def far_kernel(rows, cols, kind, *refs):
    last, weight, outs, order = refs[1], refs[2], refs[-1 - 2 * col_split(cols)[1] : -1], refs[-1]
    held = last.shape[0]
    order[pl.ds(row_of(rows, cols, rows // 2, held), held), :] = last[...]
    terms_of(order[cols * held :, :], weight, outs, kind)


def far_terms(rows, cols, order, last, weight, kind, begun=()):
    shapes = terms_shapes(cols, last.shape[0], weight.shape[0])
    aliases = {0: len(shapes)} | {3 + n: n for n in range(len(begun))}
    found = pl.pallas_call(
        functools.partial(far_kernel, rows, cols, kind),
        in_specs=[HERE] * (3 + len(begun)),
        out_specs=[HERE] * (len(shapes) + 1),
        out_shape=shapes + [jax.ShapeDtypeStruct(order.shape, order.dtype)],
        input_output_aliases=aliases,
        compiler_params=pltpu.CompilerParams(vmem_limit_bytes=VMEM_LIMIT),
    )(order, last, weight, *begun)
    return found[:-1], found[-1]


def coded(total):
    most = jnp.max(jnp.abs(total), axis=1, keepdims=True)
    exponent = jnp.ceil(jnp.log2(jnp.maximum(most, TINY)) + 1e-3)
    steps = jnp.round(total * (LEVELS / jnp.exp2(exponent))).astype(jnp.int32)
    first = steps[:, :LANES]
    lane = lax.broadcasted_iota(jnp.int32, first.shape, 1)
    shown = jnp.broadcast_to(exponent.astype(jnp.int32) + LOWEST, first.shape)
    bit = lax.shift_right_logical(shown, jnp.minimum(lane, BITS)) & 1
    first = jnp.where(lane < BITS, (first & -2) | bit, first)
    return first.astype(jnp.int16), steps[:, LANES:].astype(jnp.int16)


def decoded(part, rows):
    first = part[rows, :LANES].astype(jnp.int32)
    lane = lax.broadcasted_iota(jnp.int32, first.shape, 1)
    bits = jnp.where(lane < BITS, lax.shift_left(first & 1, jnp.minimum(lane, BITS)), 0)
    exponent = jnp.sum(bits.astype(jnp.float32), axis=1, keepdims=True) - LOWEST
    return part[rows, :].astype(jnp.float32) * (jnp.exp2(exponent) / LEVELS)


def sum_kernel(*refs):
    others = refs[0].shape[0]
    parts, outs = refs[:-others], refs[-others:]
    for k, out in enumerate(outs):
        total = parts[0][k]
        for part in parts[1:]:
            total = total + part[k]
        out[:, :LANES], out[:, LANES:] = coded(total)


def coded_sums(parts):
    others, rows, width = parts[0].shape
    return pl.pallas_call(
        sum_kernel,
        in_specs=[HERE] * len(parts),
        out_specs=[HERE] * others,
        out_shape=[jax.ShapeDtypeStruct((rows, width), jnp.int16)] * others,
        compiler_params=pltpu.CompilerParams(vmem_limit_bytes=VMEM_LIMIT),
    )(*parts)


def gate_kernel(rows, cols, near, far, *refs):
    rounds, (active, *outs) = refs[:-3], refs[-3:]
    rounds = rounds[: near + far], rounds[near + far :]
    held = active.shape[0] // PAIR
    here, col = on_ring(lax.axis_index("row"), rows), lax.axis_index("col")
    first = apart(here, on_ring(PAIR * col, rows), rows)
    second = apart(here, on_ring(PAIR * col + 1, rows), rows)
    halves = lax.select(first < second, 0, 1), lax.select(first < second, 1, 0)
    for half, parts in zip(halves, rounds):
        span = pl.ds(pl.multiple_of(half * held, held), held)
        gate = active[span, :].astype(jnp.float32)
        for n, out in enumerate(outs):
            mine = slice(n * held, (n + 1) * held)
            total = parts[0][mine, :]
            for part in parts[1:near]:
                total = total + part[mine, :]
            for part in parts[near:]:
                total = total + decoded(part, mine)
            out[span, :] = gate * total


def gated(rows, cols, rounds, active):
    near, far = rounds[0]
    parts = [part for found in rounds for kind in found for part in kind]
    size = active.size
    return pl.pallas_call(
        functools.partial(gate_kernel, rows, cols, len(near), len(far)),
        in_specs=[HERE] * (len(parts) + 1),
        out_specs=[HERE] * 2,
        out_shape=[jax.ShapeDtypeStruct(active.shape, jnp.float32)] * 2,
        compiler_params=pltpu.CompilerParams(vmem_limit_bytes=VMEM_LIMIT),
    )(*parts, active)


def parts_kernel(weight, *refs):
    magnitude, sign = refs[-2:]
    tile = min(256, weight.shape[0])
    for start in range(0, weight.shape[0], tile):
        span = slice(start, start + tile)
        w = weight[span, :].astype(jnp.float32)
        magnitude[span, :] = jnp.abs(w).astype(jnp.bfloat16)
        sign[span, :] = jnp.where(w > 0, 1.0, jnp.where(w < 0, -1.0, 0.0)).astype(jnp.bfloat16)


def parts_of(weight, *held):
    return pl.pallas_call(
        parts_kernel,
        in_specs=[HERE] * (1 + len(held)),
        out_specs=[HERE] * 2,
        out_shape=[jax.ShapeDtypeStruct(weight.shape, weight.dtype)] * 2,
        compiler_params=pltpu.CompilerParams(vmem_limit_bytes=VMEM_LIMIT),
    )(weight, *held)


def pack_kernel(first, second, out, both, sems):
    rows = first.shape[0]
    spans = [pl.ds(0, rows), pl.ds(rows, rows)]
    copies = [
        pltpu.make_async_copy(source, both.at[span, :], sem)
        for source, span, sem in zip((first, second), spans, (sems.at[0], sems.at[1]))
    ]
    onward = [
        pltpu.make_async_copy(both.at[span, :], out.at[span, :], sem)
        for span, sem in zip(spans, (sems.at[2], sems.at[3]))
    ]
    for copy in copies:
        copy.start()
    for copy, then in zip(copies, onward):
        copy.wait()
        then.start()
    for then in onward:
        then.wait()


def packed(first, second):
    rows, width = first.shape
    return pl.pallas_call(
        pack_kernel,
        in_specs=[ANYWHERE] * 2,
        out_specs=ANYWHERE,
        out_shape=jax.ShapeDtypeStruct((2 * rows, width), first.dtype),
        scratch_shapes=[pltpu.VMEM((2 * rows, width), first.dtype), pltpu.SemaphoreType.DMA((4,))],
        compiler_params=pltpu.CompilerParams(vmem_limit_bytes=VMEM_MOST),
    )(first, second)


def pack_kernel(first, second, out, both, sems):
    rows = first.shape[0]
    spans = [pl.ds(0, rows), pl.ds(rows, rows)]
    copies = [
        pltpu.make_async_copy(source, both.at[span, :], sem)
        for source, span, sem in zip((first, second), spans, (sems.at[0], sems.at[1]))
    ]
    onward = [
        pltpu.make_async_copy(both.at[span, :], out.at[span, :], sem)
        for span, sem in zip(spans, (sems.at[2], sems.at[3]))
    ]
    for copy in copies:
        copy.start()
    for copy, then in zip(copies, onward):
        copy.wait()
        then.start()
    for then in onward:
        then.wait()


def packed(first, second):
    rows, width = first.shape
    return pl.pallas_call(
        pack_kernel,
        in_specs=[ANYWHERE] * 2,
        out_specs=ANYWHERE,
        out_shape=jax.ShapeDtypeStruct((2 * rows, width), first.dtype),
        scratch_shapes=[pltpu.VMEM((2 * rows, width), first.dtype), pltpu.SemaphoreType.DMA((4,))],
        compiler_params=pltpu.CompilerParams(vmem_limit_bytes=VMEM_MOST),
    )(first, second)


def stack_kernel(*refs):
    *parts, out = refs
    rows = parts[0].shape[0]
    for n, part in enumerate(parts):
        out[n * rows : (n + 1) * rows, :] = part[...]


def stacked(parts):
    rows, width = parts[0].shape
    return pl.pallas_call(
        stack_kernel,
        in_specs=[HERE] * len(parts),
        out_specs=HERE,
        out_shape=jax.ShapeDtypeStruct((len(parts) * rows, width), parts[0].dtype),
        compiler_params=pltpu.CompilerParams(vmem_limit_bytes=VMEM_LIMIT),
    )(*parts)


def turn_kernel(rows, cols, *refs):
    held, outs, whole, order = refs[:cols], refs[cols:-2], refs[-2], refs[-1]
    owned = whole.shape[0] // cols
    shard = owned // PAIR
    for kind, out in enumerate(outs):
        for n, ref in enumerate(held):
            whole[n * owned : (n + 1) * owned, :] = ref[kind * owned : (kind + 1) * owned, :]
        for shift in by_distance(rows):
            piece, half, _ = spot(rows, cols, shift)
            start = pl.multiple_of((piece * PAIR + half) * shard, shard)
            to = row_of(rows, cols, shift, shard)
            order[pl.ds(to, shard), :] = whole[pl.ds(start, shard), :]
        out[...] = order[...].T


def turned(rows, cols, held):
    both, inner = held[0].shape
    tokens = both // 2 * cols
    return pl.pallas_call(
        functools.partial(turn_kernel, rows, cols),
        in_specs=[HERE] * cols,
        out_specs=[HERE] * 2,
        out_shape=[jax.ShapeDtypeStruct((inner, tokens), jnp.bfloat16)] * 2,
        scratch_shapes=[pltpu.VMEM((tokens, inner), jnp.bfloat16)] * 2,
        compiler_params=pltpu.CompilerParams(vmem_limit_bytes=VMEM_LIMIT),
    )(*held)


def weight_kernel(scale, center, radius, grad_c, grad_r, sign, out, parts, sems):
    tile = parts.shape[2]
    spans = [slice(start, start + tile) for start in range(0, out.shape[1], tile)]
    copies = []

    def products(span):
        return [
            lax.dot_general(ref[...], grad[:, span], BY_TOKEN, preferred_element_type=jnp.float32)
            for ref, grad in ((center, grad_c), (radius, grad_r))
        ]

    ahead = products(spans[0])
    for n, span in enumerate(spans):
        through_center, through_radius = ahead
        if n + 1 < len(spans):
            ahead = products(spans[n + 1])
        part, sem = parts.at[n % 2], sems.at[n % 2]
        if n >= 2:
            copies[n - 2].wait()
        signed = sign[:, span].astype(jnp.float32) * through_radius
        part[...] = (through_center + signed) * scale
        copies.append(pltpu.make_async_copy(part, out.at[:, pl.ds(n * tile, tile)], sem))
        copies[n].start()
    for copy in copies[-2:]:
        copy.wait()


def weight_terms(inputs, grads, sign):
    inner, width = sign.shape
    tile = min(256, width)
    scale = np.float32(1.0) / np.sqrt(np.float32(grads[0].shape[0]))
    return pl.pallas_call(
        functools.partial(weight_kernel, scale),
        in_specs=[HERE] * 5,
        out_specs=ANYWHERE,
        out_shape=jax.ShapeDtypeStruct((inner, width), jnp.float32),
        scratch_shapes=[pltpu.VMEM((2, inner, tile), jnp.float32), pltpu.SemaphoreType.DMA((2,))],
        compiler_params=pltpu.CompilerParams(vmem_limit_bytes=VMEM_LIMIT),
    )(*inputs, *grads, sign)


def on_device(rows, cols, center, radius, grad_center, grad_radius, weight, active):
    chips, cores = col_split(cols)
    held = grad_center.shape[0]
    assert rows % 2 == 0 and center.shape[0] == PAIR * held
    ring = ring_of(rows)
    clockwise = [(ring[i], ring[(i + 1) % rows]) for i in range(rows)]
    counter = [(b, a) for a, b in clockwise]
    last = rows // 2

    def swap_cores(value, j):
        perm = [(i, i - i % cores + (i % cores + j) % cores) for i in range(cols)]
        return lax.ppermute(value, "col", perm)

    def hop_chips(value, k):
        return lax.ppermute(value, "col", [(i, (i + k * cores) % cols) for i in range(cols)])

    def summed(terms):
        own, others = ([found[0]] + [swap_cores(found[j], j) for j in range(1, cores)]
                       for found in (terms[:cores], terms[cores:]))
        return own, [hop_chips(value, k + 1) for k, value in enumerate(coded_sums(others))]

    both = packed(center, radius)
    inputs = [both] + [hop_chips(both, -k) for k in range(1, chips)]
    slots_c, slots_r = {0: grad_center}, {0: grad_radius}
    shifts = by_distance(rows)
    for step in range(1, last):
        for slots in (slots_c, slots_r):
            slots[step] = lax.ppermute(slots[step - 1], "row", clockwise)
            slots[-step] = lax.ppermute(slots[1 - step], "row", counter)
    magnitude, sign = parts_of(weight, grad_center, grad_radius)
    slots_r[1 - last], weight, magnitude = lax.optimization_barrier(
        (slots_r[1 - last], weight, magnitude)
    )
    lasts = (
        lax.ppermute(slots_c[last - 1], "row", clockwise),
        lax.ppermute(slots_r[1 - last], "row", counter),
    )
    found = shifts[:-1]
    slots_c[0], inputs = lax.optimization_barrier((slots_c[0], inputs))
    terms, order_c = near_terms(rows, cols, found, [slots_c[s] for s in found], weight, 0)
    terms, order_r = near_terms(
        rows, cols, found, [slots_r[s] for s in found], magnitude, 1, terms
    )
    near = summed(terms)
    terms, order_c = far_terms(rows, cols, order_c, lasts[0], weight, 0)
    terms, order_r = far_terms(rows, cols, order_r, lasts[1], magnitude, 1, terms)
    far = summed(terms)
    orders = order_c, order_r
    inputs, _ = lax.optimization_barrier((inputs, orders))
    for j in range(1, cores):
        inputs += [swap_cores(value, -j) for value in inputs[:chips]]
    weight_grad = weight_terms(turned(rows, cols, inputs), orders, sign)
    return *gated(rows, cols, (near, far), active), weight_grad


def solution(mesh):
    spec_in, spec_out, spec_weight = P("col", "row"), P("row", "col"), P("row", "col")
    return jax.shard_map(
        functools.partial(on_device, mesh.shape["row"], mesh.shape["col"]),
        mesh=mesh,
        in_specs=(spec_in, spec_in, spec_out, spec_out, spec_weight, spec_in),
        out_specs=(spec_in, spec_in, spec_weight),
        check_vma=False,
    )
```

```python
import functools

import jax
import jax.numpy as jnp
import numpy as np
from jax import lax
from jax.experimental import pallas as pl
from jax.experimental.pallas import tpu as pltpu
from jax.sharding import PartitionSpec as P

VMEM_LIMIT = 24 * 1024 * 1024
VMEM_MOST = 60 * 1024 * 1024
HERE = pl.BlockSpec(memory_space=pltpu.VMEM)
LANES = 128
BITS, LOWEST = 8, 100
LEVELS = np.float32(32000)
TINY = np.float32(2.0**-100)
ANYWHERE = pl.BlockSpec(memory_space=pl.ANY)
BY_LAST = (((1,), (1,)), ((), ()))
BY_TOKEN = (((1,), (0,)), ((), ()))
PAIR = 2
BUFFERS = 4


def ring_of(rows):
    return list(range(0, rows, PAIR)) + list(range(rows - 1, 0, -PAIR))


def on_ring(row, rows):
    return lax.select(lax.rem(row, PAIR) == 0, lax.div(row, PAIR), rows - 1 - lax.div(row, PAIR))


def off_ring(place, rows):
    return lax.select(place < rows // PAIR, PAIR * place, PAIR * (rows - place) - 1)


def apart(a, b, rows):
    ahead = lax.rem(a - b + rows, rows)
    return lax.min(ahead, rows - ahead)


def by_distance(rows):
    return [0] + [way * step for step in range(1, rows // 2) for way in (1, -1)] + [rows // 2]


def col_split(cols):
    return (cols // 2, 2) if cols % 2 == 0 else (cols, 1)


def spot(rows, cols, shift):
    chips, cores = col_split(cols)
    here, col = on_ring(lax.axis_index("row"), rows), lax.axis_index("col")
    x, core = lax.div(col, cores), lax.rem(col, cores)
    place = lax.rem(here + (rows - shift) % rows, rows)
    source = off_ring(place, rows)
    owner, half = lax.div(source, PAIR), lax.rem(source, PAIR)
    away = lax.rem(lax.rem(owner, cores) + cores - core, cores)
    piece = away * chips + lax.rem(lax.div(owner, cores) + chips - x, chips)
    return piece, half, abs(shift) > apart(here, rows - 1 - place, rows)


def row_of(rows, cols, shift, held):
    piece, _, far = spot(rows, cols, shift)
    return pl.multiple_of((lax.select(far, cols, 0) + piece) * held, held)


def terms_of(lhs, weight, outs, kind):
    cores, chips = len(outs), outs[0].shape[0]
    inner = weight.shape[0]
    tile = min(1024, inner)
    held = lhs.shape[0] // (cores * chips)
    rows = slice(kind * held, (kind + 1) * held)
    for i in range(inner // tile):
        span = slice(i * tile, (i + 1) * tile)
        terms = lax.dot_general(
            lhs, weight[span, :], BY_LAST, preferred_element_type=jnp.float32
        )
        for n in range(cores * chips):
            core, chip = divmod(n, chips)
            outs[core][chip, rows, span] = terms[n * held : (n + 1) * held, :]


def terms_shapes(cols, held, inner):
    chips, cores = col_split(cols)
    return [jax.ShapeDtypeStruct((chips, 2 * held, inner), jnp.float32)] * cores


def near_kernel(rows, cols, shifts, kind, *refs):
    count = len(shifts)
    slots, weight, outs, order = refs[:count], refs[count], refs[-1 - col_split(cols)[1] : -1], refs[-1]
    held = slots[0].shape[0]
    for shift, slot in zip(shifts, slots):
        order[pl.ds(row_of(rows, cols, shift, held), held), :] = slot[...]
    terms_of(order[: cols * held, :], weight, outs, kind)


def near_terms(rows, cols, shifts, slots, weight, kind, begun=()):
    inner, width = weight.shape
    held = slots[0].shape[0]
    shapes = terms_shapes(cols, held, inner)
    found = pl.pallas_call(
        functools.partial(near_kernel, rows, cols, shifts, kind),
        in_specs=[HERE] * (len(slots) + 1 + len(begun)),
        out_specs=[HERE] * (len(shapes) + 1),
        out_shape=shapes + [jax.ShapeDtypeStruct((held * rows, width), jnp.bfloat16)],
        input_output_aliases={len(slots) + 1 + n: n for n in range(len(begun))},
        compiler_params=pltpu.CompilerParams(vmem_limit_bytes=VMEM_LIMIT),
    )(*slots, weight, *begun)
    return found[:-1], found[-1]


def far_kernel(rows, cols, kind, *refs):
    last, weight, outs, order = refs[1], refs[2], refs[-1 - col_split(cols)[1] : -1], refs[-1]
    held = last.shape[0]
    order[pl.ds(row_of(rows, cols, rows // 2, held), held), :] = last[...]
    terms_of(order[cols * held :, :], weight, outs, kind)


def far_terms(rows, cols, order, last, weight, kind, begun=()):
    shapes = terms_shapes(cols, last.shape[0], weight.shape[0])
    aliases = {0: len(shapes)} | {3 + n: n for n in range(len(begun))}
    found = pl.pallas_call(
        functools.partial(far_kernel, rows, cols, kind),
        in_specs=[HERE] * (3 + len(begun)),
        out_specs=[HERE] * (len(shapes) + 1),
        out_shape=shapes + [jax.ShapeDtypeStruct(order.shape, order.dtype)],
        input_output_aliases=aliases,
        compiler_params=pltpu.CompilerParams(vmem_limit_bytes=VMEM_LIMIT),
    )(order, last, weight, *begun)
    return found[:-1], found[-1]


def coded(total):
    most = jnp.max(jnp.abs(total), axis=1, keepdims=True)
    exponent = jnp.ceil(jnp.log2(jnp.maximum(most, TINY)) + 1e-3)
    steps = jnp.round(total * (LEVELS / jnp.exp2(exponent))).astype(jnp.int32)
    first = steps[:, :LANES]
    lane = lax.broadcasted_iota(jnp.int32, first.shape, 1)
    shown = jnp.broadcast_to(exponent.astype(jnp.int32) + LOWEST, first.shape)
    bit = lax.shift_right_logical(shown, jnp.minimum(lane, BITS)) & 1
    first = jnp.where(lane < BITS, (first & -2) | bit, first)
    return first.astype(jnp.int16), steps[:, LANES:].astype(jnp.int16)


def decoded(part, rows):
    first = part[rows, :LANES].astype(jnp.int32)
    lane = lax.broadcasted_iota(jnp.int32, first.shape, 1)
    bits = jnp.where(lane < BITS, lax.shift_left(first & 1, jnp.minimum(lane, BITS)), 0)
    exponent = jnp.sum(bits.astype(jnp.float32), axis=1, keepdims=True) - LOWEST
    return part[rows, :].astype(jnp.float32) * (jnp.exp2(exponent) / LEVELS)


def sum_kernel(*refs):
    others = refs[0].shape[0] - 1
    parts, outs = refs[:-others], refs[-others:]
    for k, out in enumerate(outs, 1):
        total = parts[0][k]
        for part in parts[1:]:
            total = total + part[k]
        out[:, :LANES], out[:, LANES:] = coded(total)


def coded_sums(parts):
    chips, rows, width = parts[0].shape
    return pl.pallas_call(
        sum_kernel,
        in_specs=[HERE] * len(parts),
        out_specs=[HERE] * (chips - 1),
        out_shape=[jax.ShapeDtypeStruct((rows, width), jnp.int16)] * (chips - 1),
        compiler_params=pltpu.CompilerParams(vmem_limit_bytes=VMEM_LIMIT),
    )(*parts)


def gate_kernel(rows, n, near, far, *refs):
    parts, active = refs[: near + far], refs[near + far]
    outs, (work, sems) = refs[-4:-2], refs[-2:]
    held = active.shape[0] // PAIR
    here, col = on_ring(lax.axis_index("row"), rows), lax.axis_index("col")
    first = apart(here, on_ring(PAIR * col, rows), rows)
    second = apart(here, on_ring(PAIR * col + 1, rows), rows)
    half = lax.select(first < second, n, 1 - n)
    span = pl.ds(pl.multiple_of(half * held, held), held)
    gate = active[span, :].astype(jnp.float32)
    copies = []
    for kind, out in enumerate(outs):
        mine = slice(kind * held, (kind + 1) * held)
        total = parts[0][0, mine, :]
        for part in parts[1:near]:
            total = total + part[0, mine, :]
        for part in parts[near:]:
            total = total + decoded(part, mine)
        work[mine, :] = gate * total
        copies.append(pltpu.make_async_copy(work.at[pl.ds(kind * held, held), :], out.at[span, :], sems.at[kind]))
        copies[kind].start()
    for copy in copies:
        copy.wait()


def gated(rows, n, found, active, begun=()):
    near, far = found
    parts = [*near, *far]
    return pl.pallas_call(
        functools.partial(gate_kernel, rows, n, len(near), len(far)),
        in_specs=[HERE] * (len(parts) + 1) + [ANYWHERE] * len(begun),
        out_specs=[ANYWHERE] * 2,
        out_shape=[jax.ShapeDtypeStruct(active.shape, jnp.float32)] * 2,
        scratch_shapes=[
            pltpu.VMEM(active.shape, jnp.float32),
            pltpu.SemaphoreType.DMA((2,)),
        ],
        input_output_aliases={len(parts) + 1 + k: k for k in range(len(begun))},
        compiler_params=pltpu.CompilerParams(vmem_limit_bytes=VMEM_LIMIT),
    )(*parts, active, *begun)


def parts_kernel(weight, *refs):
    magnitude, sign = refs[-2:]
    tile = min(256, weight.shape[0])
    for start in range(0, weight.shape[0], tile):
        span = slice(start, start + tile)
        w = weight[span, :]
        one = jnp.ones_like(w)
        magnitude[span, :] = jnp.abs(w)
        sign[span, :] = jnp.where(w > 0, one, jnp.where(w < 0, -one, jnp.zeros_like(w)))


def parts_of(weight, *held):
    return pl.pallas_call(
        parts_kernel,
        in_specs=[HERE] * (1 + len(held)),
        out_specs=[HERE] * 2,
        out_shape=[jax.ShapeDtypeStruct(weight.shape, weight.dtype)] * 2,
        compiler_params=pltpu.CompilerParams(vmem_limit_bytes=VMEM_LIMIT),
    )(weight, *held)


def pack_kernel(first, second, out, both, sems):
    rows = first.shape[0]
    spans = [pl.ds(0, rows), pl.ds(rows, rows)]
    copies = [
        pltpu.make_async_copy(source, both.at[span, :], sem)
        for source, span, sem in zip((first, second), spans, (sems.at[0], sems.at[1]))
    ]
    onward = [
        pltpu.make_async_copy(both.at[span, :], out.at[span, :], sem)
        for span, sem in zip(spans, (sems.at[2], sems.at[3]))
    ]
    for copy in copies:
        copy.start()
    for copy, then in zip(copies, onward):
        copy.wait()
        then.start()
    for then in onward:
        then.wait()


def packed(first, second):
    rows, width = first.shape
    return pl.pallas_call(
        pack_kernel,
        in_specs=[ANYWHERE] * 2,
        out_specs=ANYWHERE,
        out_shape=jax.ShapeDtypeStruct((2 * rows, width), first.dtype),
        scratch_shapes=[pltpu.VMEM((2 * rows, width), first.dtype), pltpu.SemaphoreType.DMA((4,))],
        compiler_params=pltpu.CompilerParams(vmem_limit_bytes=VMEM_MOST),
    )(first, second)


def pack_kernel(first, second, out, both, sems):
    rows = first.shape[0]
    spans = [pl.ds(0, rows), pl.ds(rows, rows)]
    copies = [
        pltpu.make_async_copy(source, both.at[span, :], sem)
        for source, span, sem in zip((first, second), spans, (sems.at[0], sems.at[1]))
    ]
    onward = [
        pltpu.make_async_copy(both.at[span, :], out.at[span, :], sem)
        for span, sem in zip(spans, (sems.at[2], sems.at[3]))
    ]
    for copy in copies:
        copy.start()
    for copy, then in zip(copies, onward):
        copy.wait()
        then.start()
    for then in onward:
        then.wait()


def packed(first, second):
    rows, width = first.shape
    return pl.pallas_call(
        pack_kernel,
        in_specs=[ANYWHERE] * 2,
        out_specs=ANYWHERE,
        out_shape=jax.ShapeDtypeStruct((2 * rows, width), first.dtype),
        scratch_shapes=[pltpu.VMEM((2 * rows, width), first.dtype), pltpu.SemaphoreType.DMA((4,))],
        compiler_params=pltpu.CompilerParams(vmem_limit_bytes=VMEM_MOST),
    )(first, second)


def stack_kernel(*refs):
    *parts, out = refs
    rows = parts[0].shape[0]
    for n, part in enumerate(parts):
        out[n * rows : (n + 1) * rows, :] = part[...]


def stacked(parts):
    rows, width = parts[0].shape
    return pl.pallas_call(
        stack_kernel,
        in_specs=[HERE] * len(parts),
        out_specs=HERE,
        out_shape=jax.ShapeDtypeStruct((len(parts) * rows, width), parts[0].dtype),
        compiler_params=pltpu.CompilerParams(vmem_limit_bytes=VMEM_LIMIT),
    )(*parts)


def turn_kernel(rows, cols, *refs):
    held, outs, whole, order = refs[:cols], refs[cols:-2], refs[-2], refs[-1]
    owned = whole.shape[0] // cols
    shard = owned // PAIR
    for kind, out in enumerate(outs):
        for n, ref in enumerate(held):
            whole[n * owned : (n + 1) * owned, :] = ref[kind * owned : (kind + 1) * owned, :]
        for shift in by_distance(rows):
            piece, half, _ = spot(rows, cols, shift)
            start = pl.multiple_of((piece * PAIR + half) * shard, shard)
            to = row_of(rows, cols, shift, shard)
            order[pl.ds(to, shard), :] = whole[pl.ds(start, shard), :]
        out[...] = order[...].T


def turned(rows, cols, held):
    both, inner = held[0].shape
    tokens = both // 2 * cols
    return pl.pallas_call(
        functools.partial(turn_kernel, rows, cols),
        in_specs=[HERE] * cols,
        out_specs=[HERE] * 2,
        out_shape=[jax.ShapeDtypeStruct((inner, tokens), jnp.bfloat16)] * 2,
        scratch_shapes=[pltpu.VMEM((tokens, inner), jnp.bfloat16)] * 2,
        compiler_params=pltpu.CompilerParams(vmem_limit_bytes=VMEM_LIMIT),
    )(*held)


def weight_kernel(scale, center, radius, grad_c, grad_r, sign, out, parts, sems):
    tile = parts.shape[2]
    copies = []
    for n in range(out.shape[1] // tile):
        span = slice(n * tile, (n + 1) * tile)
        part, sem = parts.at[n % BUFFERS], sems.at[n % BUFFERS]
        if n >= BUFFERS:
            copies[n - BUFFERS].wait()
        through_center, through_radius = (
            lax.dot_general(ref[...], grad[:, span], BY_TOKEN, preferred_element_type=jnp.float32)
            for ref, grad in ((center, grad_c), (radius, grad_r))
        )
        signed = sign[:, span].astype(jnp.float32) * through_radius
        part[...] = (through_center + signed) * scale
        copies.append(pltpu.make_async_copy(part, out.at[:, pl.ds(n * tile, tile)], sem))
        copies[n].start()
    for copy in copies[-BUFFERS:]:
        copy.wait()


def weight_terms(inputs, grads, sign):
    inner, width = sign.shape
    tile = min(256, width)
    scale = np.float32(1.0) / np.sqrt(np.float32(grads[0].shape[0]))
    return pl.pallas_call(
        functools.partial(weight_kernel, scale),
        in_specs=[HERE] * 5,
        out_specs=ANYWHERE,
        out_shape=jax.ShapeDtypeStruct((inner, width), jnp.float32),
        scratch_shapes=[
            pltpu.VMEM((BUFFERS, inner, tile), jnp.float32),
            pltpu.SemaphoreType.DMA((BUFFERS,)),
        ],
        compiler_params=pltpu.CompilerParams(vmem_limit_bytes=VMEM_LIMIT),
    )(*inputs, *grads, sign)


def on_device(rows, cols, center, radius, grad_center, grad_radius, weight, active):
    chips, cores = col_split(cols)
    held = grad_center.shape[0]
    assert rows % 2 == 0 and center.shape[0] == PAIR * held
    ring = ring_of(rows)
    clockwise = [(ring[i], ring[(i + 1) % rows]) for i in range(rows)]
    counter = [(b, a) for a, b in clockwise]
    last = rows // 2

    def swap_cores(value, j):
        perm = [(i, i - i % cores + (i % cores + j) % cores) for i in range(cols)]
        return lax.ppermute(value, "col", perm)

    def hop_chips(value, k):
        return lax.ppermute(value, "col", [(i, (i + k * cores) % cols) for i in range(cols)])

    def summed(terms):
        parts = [terms[0]] + [swap_cores(terms[j], j) for j in range(1, cores)]
        return parts, [hop_chips(value, k + 1) for k, value in enumerate(coded_sums(parts))]

    both = packed(center, radius)
    inputs = [both] + [hop_chips(both, -k) for k in range(1, chips)]
    slots_c, slots_r = {0: grad_center}, {0: grad_radius}
    shifts = by_distance(rows)
    for step in range(1, last):
        for slots in (slots_c, slots_r):
            slots[step] = lax.ppermute(slots[step - 1], "row", clockwise)
            slots[-step] = lax.ppermute(slots[1 - step], "row", counter)
    magnitude, sign = parts_of(weight)
    slots_r[1 - last], weight, magnitude = lax.optimization_barrier(
        (slots_r[1 - last], weight, magnitude)
    )
    lasts = (
        lax.ppermute(slots_c[last - 1], "row", clockwise),
        lax.ppermute(slots_r[1 - last], "row", counter),
    )
    found = shifts[:-1]
    slots_c[0], inputs = lax.optimization_barrier((slots_c[0], inputs))
    terms, order_c = near_terms(rows, cols, found, [slots_c[s] for s in found], weight, 0)
    terms, order_r = near_terms(
        rows, cols, found, [slots_r[s] for s in found], magnitude, 1, terms
    )
    near = summed(terms)
    terms, order_c = far_terms(rows, cols, order_c, lasts[0], weight, 0)
    terms, order_r = far_terms(rows, cols, order_r, lasts[1], magnitude, 1, terms)
    far = summed(terms)
    inputs, _ = lax.optimization_barrier((inputs, (order_c, order_r)))
    for j in range(1, cores):
        inputs += [swap_cores(value, -j) for value in inputs[:chips]]
    inputs = turned(rows, cols, inputs)
    weight_grad = weight_terms(inputs, (order_c, order_r), sign)
    begun = gated(rows, 0, near, active)
    return *gated(rows, 1, far, active, begun), weight_grad


def solution(mesh):
    spec_in, spec_out, spec_weight = P("col", "row"), P("row", "col"), P("row", "col")
    return jax.shard_map(
        functools.partial(on_device, mesh.shape["row"], mesh.shape["col"]),
        mesh=mesh,
        in_specs=(spec_in, spec_in, spec_out, spec_out, spec_weight, spec_in),
        out_specs=(spec_in, spec_in, spec_weight),
        check_vma=False,
    )
```

```python
import functools

import jax
import jax.numpy as jnp
import numpy as np
from jax import lax
from jax.experimental import pallas as pl
from jax.experimental.pallas import tpu as pltpu
from jax.sharding import PartitionSpec as P

VMEM_LIMIT = 24 * 1024 * 1024
VMEM_MOST = 60 * 1024 * 1024
HERE = pl.BlockSpec(memory_space=pltpu.VMEM)
LANES = 128
BITS, LOWEST = 8, 100
LEVELS = np.float32(32000)
TINY = np.float32(2.0**-100)
ANYWHERE = pl.BlockSpec(memory_space=pl.ANY)
BY_LAST = (((1,), (1,)), ((), ()))
BY_TOKEN = (((1,), (0,)), ((), ()))
PAIR = 2
BUFFERS = 4
BLOCKS = 2


def ring_of(rows):
    return list(range(0, rows, PAIR)) + list(range(rows - 1, 0, -PAIR))


def on_ring(row, rows):
    return lax.select(lax.rem(row, PAIR) == 0, lax.div(row, PAIR), rows - 1 - lax.div(row, PAIR))


def off_ring(place, rows):
    return lax.select(place < rows // PAIR, PAIR * place, PAIR * (rows - place) - 1)


def apart(a, b, rows):
    ahead = lax.rem(a - b + rows, rows)
    return lax.min(ahead, rows - ahead)


def by_distance(rows):
    return [0] + [way * step for step in range(1, rows // 2) for way in (1, -1)] + [rows // 2]


def col_split(cols):
    return (cols // 2, 2) if cols % 2 == 0 else (cols, 1)


def spot(rows, cols, shift):
    chips, cores = col_split(cols)
    here, col = on_ring(lax.axis_index("row"), rows), lax.axis_index("col")
    x, core = lax.div(col, cores), lax.rem(col, cores)
    place = lax.rem(here + (rows - shift) % rows, rows)
    source = off_ring(place, rows)
    owner, half = lax.div(source, PAIR), lax.rem(source, PAIR)
    away = lax.rem(lax.rem(owner, cores) + cores - core, cores)
    piece = away * chips + lax.rem(lax.div(owner, cores) + chips - x, chips)
    return piece, half, abs(shift) > apart(here, rows - 1 - place, rows)


def row_of(rows, cols, shift, held):
    piece, _, far = spot(rows, cols, shift)
    return pl.multiple_of((lax.select(far, cols, 0) + piece) * held, held)


def terms_of(lhs, weight, outs, kind):
    cores, chips = len(outs), outs[0].shape[0]
    inner = weight.shape[0]
    tile = min(256, inner)
    held = lhs.shape[0] // (cores * chips)
    rows = slice(kind * held, (kind + 1) * held)
    for i in range(inner // tile):
        span = slice(i * tile, (i + 1) * tile)
        terms = lax.dot_general(
            lhs, weight[span, :], BY_LAST, preferred_element_type=jnp.float32
        )
        for n in range(cores * chips):
            core, chip = divmod(n, chips)
            outs[core][chip, rows, span] = terms[n * held : (n + 1) * held, :]


def terms_shapes(cols, held, inner):
    chips, cores = col_split(cols)
    return [jax.ShapeDtypeStruct((chips, 2 * held, inner), jnp.float32)] * cores


def near_kernel(rows, cols, shifts, kind, *refs):
    count = len(shifts)
    slots, weight, outs, order = refs[:count], refs[count], refs[-1 - col_split(cols)[1] : -1], refs[-1]
    held = slots[0].shape[0]
    for shift, slot in zip(shifts, slots):
        order[pl.ds(row_of(rows, cols, shift, held), held), :] = slot[...]
    terms_of(order[: cols * held, :], weight, outs, kind)


def near_terms(rows, cols, shifts, slots, weight, kind, begun=()):
    inner, width = weight.shape
    held = slots[0].shape[0]
    shapes = terms_shapes(cols, held, inner)
    found = pl.pallas_call(
        functools.partial(near_kernel, rows, cols, shifts, kind),
        in_specs=[HERE] * (len(slots) + 1 + len(begun)),
        out_specs=[HERE] * (len(shapes) + 1),
        out_shape=shapes + [jax.ShapeDtypeStruct((held * rows, width), jnp.bfloat16)],
        input_output_aliases={len(slots) + 1 + n: n for n in range(len(begun))},
        compiler_params=pltpu.CompilerParams(vmem_limit_bytes=VMEM_LIMIT),
    )(*slots, weight, *begun)
    return found[:-1], found[-1]


def far_kernel(rows, cols, kind, *refs):
    last, weight, outs, order = refs[1], refs[2], refs[-1 - col_split(cols)[1] : -1], refs[-1]
    held = last.shape[0]
    order[pl.ds(row_of(rows, cols, rows // 2, held), held), :] = last[...]
    terms_of(order[cols * held :, :], weight, outs, kind)


def far_terms(rows, cols, order, last, weight, kind, begun=()):
    shapes = terms_shapes(cols, last.shape[0], weight.shape[0])
    aliases = {0: len(shapes)} | {3 + n: n for n in range(len(begun))}
    found = pl.pallas_call(
        functools.partial(far_kernel, rows, cols, kind),
        in_specs=[HERE] * (3 + len(begun)),
        out_specs=[HERE] * (len(shapes) + 1),
        out_shape=shapes + [jax.ShapeDtypeStruct(order.shape, order.dtype)],
        input_output_aliases=aliases,
        compiler_params=pltpu.CompilerParams(vmem_limit_bytes=VMEM_LIMIT),
    )(order, last, weight, *begun)
    return found[:-1], found[-1]


def coded(total):
    most = jnp.max(jnp.abs(total), axis=1, keepdims=True)
    exponent = jnp.ceil(jnp.log2(jnp.maximum(most, TINY)) + 1e-3)
    steps = jnp.round(total * (LEVELS / jnp.exp2(exponent))).astype(jnp.int32)
    first = steps[:, :LANES]
    lane = lax.broadcasted_iota(jnp.int32, first.shape, 1)
    shown = jnp.broadcast_to(exponent.astype(jnp.int32) + LOWEST, first.shape)
    bit = lax.shift_right_logical(shown, jnp.minimum(lane, BITS)) & 1
    first = jnp.where(lane < BITS, (first & -2) | bit, first)
    return first.astype(jnp.int16), steps[:, LANES:].astype(jnp.int16)


def decoded(part, rows):
    first = part[rows, :LANES].astype(jnp.int32)
    lane = lax.broadcasted_iota(jnp.int32, first.shape, 1)
    bits = jnp.where(lane < BITS, lax.shift_left(first & 1, jnp.minimum(lane, BITS)), 0)
    exponent = jnp.sum(bits.astype(jnp.float32), axis=1, keepdims=True) - LOWEST
    return part[rows, :].astype(jnp.float32) * (jnp.exp2(exponent) / LEVELS)


def sum_kernel(*refs):
    others = refs[0].shape[0] - 1
    parts, outs = refs[:-others], refs[-others:]
    for k, out in enumerate(outs, 1):
        total = parts[0][k]
        for part in parts[1:]:
            total = total + part[k]
        out[:, :LANES], out[:, LANES:] = coded(total)


def coded_sums(parts):
    chips, rows, width = parts[0].shape
    return pl.pallas_call(
        sum_kernel,
        in_specs=[HERE] * len(parts),
        out_specs=[HERE] * (chips - 1),
        out_shape=[jax.ShapeDtypeStruct((rows, width), jnp.int16)] * (chips - 1),
        compiler_params=pltpu.CompilerParams(vmem_limit_bytes=VMEM_LIMIT),
    )(*parts)


def gate_kernel(rows, n, near, far, *refs):
    parts, active = refs[: near + far], refs[near + far]
    outs, (work, sems) = refs[-4:-2], refs[-2:]
    held = active.shape[0] // PAIR
    here, col = on_ring(lax.axis_index("row"), rows), lax.axis_index("col")
    first = apart(here, on_ring(PAIR * col, rows), rows)
    second = apart(here, on_ring(PAIR * col + 1, rows), rows)
    half = lax.select(first < second, n, 1 - n)
    span = pl.ds(pl.multiple_of(half * held, held), held)
    gate = active[span, :].astype(jnp.float32)
    copies = []
    block = held // BLOCKS
    for kind, out in enumerate(outs):
        for i in range(BLOCKS):
            first = kind * held + i * block
            mine = slice(first, first + block)
            total = parts[0][0, mine, :]
            for part in parts[1:near]:
                total = total + part[0, mine, :]
            for part in parts[near:]:
                total = total + decoded(part, mine)
            work[mine, :] = gate[i * block : (i + 1) * block, :] * total
            to = pl.ds(pl.multiple_of(half * held + i * block, block), block)
            copy = pltpu.make_async_copy(
                work.at[pl.ds(first, block), :], out.at[to, :], sems.at[kind * BLOCKS + i]
            )
            copy.start()
            copies.append(copy)
    for copy in copies:
        copy.wait()


def gated(rows, n, found, active, begun=()):
    near, far = found
    parts = [*near, *far]
    return pl.pallas_call(
        functools.partial(gate_kernel, rows, n, len(near), len(far)),
        in_specs=[HERE] * (len(parts) + 1) + [ANYWHERE] * len(begun),
        out_specs=[ANYWHERE] * 2,
        out_shape=[jax.ShapeDtypeStruct(active.shape, jnp.float32)] * 2,
        scratch_shapes=[
            pltpu.VMEM(active.shape, jnp.float32),
            pltpu.SemaphoreType.DMA((2 * BLOCKS,)),
        ],
        input_output_aliases={len(parts) + 1 + k: k for k in range(len(begun))},
        compiler_params=pltpu.CompilerParams(vmem_limit_bytes=VMEM_LIMIT),
    )(*parts, active, *begun)


def parts_kernel(weight, *refs):
    magnitude, sign = refs[-2:]
    tile = min(256, weight.shape[0])
    for start in range(0, weight.shape[0], tile):
        span = slice(start, start + tile)
        w = weight[span, :]
        one = jnp.ones_like(w)
        magnitude[span, :] = jnp.abs(w)
        sign[span, :] = jnp.where(w > 0, one, jnp.where(w < 0, -one, jnp.zeros_like(w)))


def parts_of(weight, *held):
    return pl.pallas_call(
        parts_kernel,
        in_specs=[HERE] * (1 + len(held)),
        out_specs=[HERE] * 2,
        out_shape=[jax.ShapeDtypeStruct(weight.shape, weight.dtype)] * 2,
        compiler_params=pltpu.CompilerParams(vmem_limit_bytes=VMEM_LIMIT),
    )(weight, *held)


def pack_kernel(first, second, out, both, sems):
    rows = first.shape[0]
    spans = [pl.ds(0, rows), pl.ds(rows, rows)]
    copies = [
        pltpu.make_async_copy(source, both.at[span, :], sem)
        for source, span, sem in zip((first, second), spans, (sems.at[0], sems.at[1]))
    ]
    onward = [
        pltpu.make_async_copy(both.at[span, :], out.at[span, :], sem)
        for span, sem in zip(spans, (sems.at[2], sems.at[3]))
    ]
    for copy in copies:
        copy.start()
    for copy, then in zip(copies, onward):
        copy.wait()
        then.start()
    for then in onward:
        then.wait()


def packed(first, second):
    rows, width = first.shape
    return pl.pallas_call(
        pack_kernel,
        in_specs=[ANYWHERE] * 2,
        out_specs=ANYWHERE,
        out_shape=jax.ShapeDtypeStruct((2 * rows, width), first.dtype),
        scratch_shapes=[pltpu.VMEM((2 * rows, width), first.dtype), pltpu.SemaphoreType.DMA((4,))],
        compiler_params=pltpu.CompilerParams(vmem_limit_bytes=VMEM_MOST),
    )(first, second)


def pack_kernel(first, second, out, both, sems):
    rows = first.shape[0]
    spans = [pl.ds(0, rows), pl.ds(rows, rows)]
    copies = [
        pltpu.make_async_copy(source, both.at[span, :], sem)
        for source, span, sem in zip((first, second), spans, (sems.at[0], sems.at[1]))
    ]
    onward = [
        pltpu.make_async_copy(both.at[span, :], out.at[span, :], sem)
        for span, sem in zip(spans, (sems.at[2], sems.at[3]))
    ]
    for copy in copies:
        copy.start()
    for copy, then in zip(copies, onward):
        copy.wait()
        then.start()
    for then in onward:
        then.wait()


def packed(first, second):
    rows, width = first.shape
    return pl.pallas_call(
        pack_kernel,
        in_specs=[ANYWHERE] * 2,
        out_specs=ANYWHERE,
        out_shape=jax.ShapeDtypeStruct((2 * rows, width), first.dtype),
        scratch_shapes=[pltpu.VMEM((2 * rows, width), first.dtype), pltpu.SemaphoreType.DMA((4,))],
        compiler_params=pltpu.CompilerParams(vmem_limit_bytes=VMEM_MOST),
    )(first, second)


def stack_kernel(*refs):
    *parts, out = refs
    rows = parts[0].shape[0]
    for n, part in enumerate(parts):
        out[n * rows : (n + 1) * rows, :] = part[...]


def stacked(parts):
    rows, width = parts[0].shape
    return pl.pallas_call(
        stack_kernel,
        in_specs=[HERE] * len(parts),
        out_specs=HERE,
        out_shape=jax.ShapeDtypeStruct((len(parts) * rows, width), parts[0].dtype),
        compiler_params=pltpu.CompilerParams(vmem_limit_bytes=VMEM_LIMIT),
    )(*parts)


def turn_kernel(rows, cols, *refs):
    held, outs, whole, order = refs[:cols], refs[cols:-2], refs[-2], refs[-1]
    owned = whole.shape[0] // cols
    shard = owned // PAIR
    for kind, out in enumerate(outs):
        for n, ref in enumerate(held):
            whole[n * owned : (n + 1) * owned, :] = ref[kind * owned : (kind + 1) * owned, :]
        for shift in by_distance(rows):
            piece, half, _ = spot(rows, cols, shift)
            start = pl.multiple_of((piece * PAIR + half) * shard, shard)
            to = row_of(rows, cols, shift, shard)
            order[pl.ds(to, shard), :] = whole[pl.ds(start, shard), :]
        out[...] = order[...].T


def turned(rows, cols, held):
    both, inner = held[0].shape
    tokens = both // 2 * cols
    return pl.pallas_call(
        functools.partial(turn_kernel, rows, cols),
        in_specs=[HERE] * cols,
        out_specs=[HERE] * 2,
        out_shape=[jax.ShapeDtypeStruct((inner, tokens), jnp.bfloat16)] * 2,
        scratch_shapes=[pltpu.VMEM((tokens, inner), jnp.bfloat16)] * 2,
        compiler_params=pltpu.CompilerParams(vmem_limit_bytes=VMEM_LIMIT),
    )(*held)


def weight_kernel(scale, center, radius, grad_c, grad_r, sign, out, parts, sems):
    tile = parts.shape[2]
    copies = []
    for n in range(out.shape[1] // tile):
        span = slice(n * tile, (n + 1) * tile)
        part, sem = parts.at[n % BUFFERS], sems.at[n % BUFFERS]
        if n >= BUFFERS:
            copies[n - BUFFERS].wait()
        through_center, through_radius = (
            lax.dot_general(ref[...], grad[:, span], BY_TOKEN, preferred_element_type=jnp.float32)
            for ref, grad in ((center, grad_c), (radius, grad_r))
        )
        signed = sign[:, span].astype(jnp.float32) * through_radius
        part[...] = (through_center + signed) * scale
        copies.append(pltpu.make_async_copy(part, out.at[:, pl.ds(n * tile, tile)], sem))
        copies[n].start()
    for copy in copies[-BUFFERS:]:
        copy.wait()


def weight_terms(inputs, grads, sign):
    inner, width = sign.shape
    tile = min(256, width)
    scale = np.float32(1.0) / np.sqrt(np.float32(grads[0].shape[0]))
    return pl.pallas_call(
        functools.partial(weight_kernel, scale),
        in_specs=[HERE] * 5,
        out_specs=ANYWHERE,
        out_shape=jax.ShapeDtypeStruct((inner, width), jnp.float32),
        scratch_shapes=[
            pltpu.VMEM((BUFFERS, inner, tile), jnp.float32),
            pltpu.SemaphoreType.DMA((BUFFERS,)),
        ],
        compiler_params=pltpu.CompilerParams(vmem_limit_bytes=VMEM_LIMIT),
    )(*inputs, *grads, sign)


def on_device(rows, cols, center, radius, grad_center, grad_radius, weight, active):
    chips, cores = col_split(cols)
    held = grad_center.shape[0]
    assert rows % 2 == 0 and center.shape[0] == PAIR * held
    ring = ring_of(rows)
    clockwise = [(ring[i], ring[(i + 1) % rows]) for i in range(rows)]
    counter = [(b, a) for a, b in clockwise]
    last = rows // 2

    def swap_cores(value, j):
        perm = [(i, i - i % cores + (i % cores + j) % cores) for i in range(cols)]
        return lax.ppermute(value, "col", perm)

    def hop_chips(value, k):
        return lax.ppermute(value, "col", [(i, (i + k * cores) % cols) for i in range(cols)])

    def summed(terms):
        parts = [terms[0]] + [swap_cores(terms[j], j) for j in range(1, cores)]
        return parts, [hop_chips(value, k + 1) for k, value in enumerate(coded_sums(parts))]

    both = packed(center, radius)
    inputs = [both] + [hop_chips(both, -k) for k in range(1, chips)]
    slots_c, slots_r = {0: grad_center}, {0: grad_radius}
    shifts = by_distance(rows)
    for step in range(1, last):
        for slots in (slots_c, slots_r):
            slots[step] = lax.ppermute(slots[step - 1], "row", clockwise)
            slots[-step] = lax.ppermute(slots[1 - step], "row", counter)
    magnitude, sign = parts_of(weight)
    slots_r[1 - last], weight, magnitude = lax.optimization_barrier(
        (slots_r[1 - last], weight, magnitude)
    )
    lasts = (
        lax.ppermute(slots_c[last - 1], "row", clockwise),
        lax.ppermute(slots_r[1 - last], "row", counter),
    )
    found = shifts[:-1]
    slots_c[0], inputs = lax.optimization_barrier((slots_c[0], inputs))
    terms, order_c = near_terms(rows, cols, found, [slots_c[s] for s in found], weight, 0)
    terms, order_r = near_terms(
        rows, cols, found, [slots_r[s] for s in found], magnitude, 1, terms
    )
    near = summed(terms)
    terms, order_c = far_terms(rows, cols, order_c, lasts[0], weight, 0)
    terms, order_r = far_terms(rows, cols, order_r, lasts[1], magnitude, 1, terms)
    far = summed(terms)
    inputs, _ = lax.optimization_barrier((inputs, (order_c, order_r)))
    for j in range(1, cores):
        inputs += [swap_cores(value, -j) for value in inputs[:chips]]
    inputs = turned(rows, cols, inputs)
    weight_grad = weight_terms(inputs, (order_c, order_r), sign)
    begun = gated(rows, 0, near, active)
    return *gated(rows, 1, far, active, begun), weight_grad


def solution(mesh):
    spec_in, spec_out, spec_weight = P("col", "row"), P("row", "col"), P("row", "col")
    return jax.shard_map(
        functools.partial(on_device, mesh.shape["row"], mesh.shape["col"]),
        mesh=mesh,
        in_specs=(spec_in, spec_in, spec_out, spec_out, spec_weight, spec_in),
        out_specs=(spec_in, spec_in, spec_weight),
        check_vma=False,
    )
```
